256 devices in a mesh: seq: 32 (over z, y), mp: 8 (over x, core).
Axes of the slice: x: 4, y: 4, z: 8, core: 2. Of those that a mesh axis runs over, the one named last changes fastest.
Arguments:
- tokens: bfloat16 [65536, 2048], P('seq'), may hold values from -6 to 6
- w_proj: bfloat16 [2048, 4, 2048], P(None, None, 'mp')
- gain: float32 [2048], P('mp'), may hold values from 0.25 to 1.75
- level_codes: int32 [11, 16, 65536], P(None, 'mp', 'seq'), may hold values from 0 to 255
- w_codes: int32 [2048, 2048], P('mp'), may hold values from 40 to 199, as said below
- block_exponent: int32 [16, 16], P('mp'), may hold values from -7 to -5
Outputs:
- mixed: bfloat16 [65536, 2048], P(('seq', 'mp'))
The draws below stay inside these ranges and needn't reach their ends.
Inputs may be any that keep to these rules, and one draw needn't show every extreme that they name: `w_codes`: each code is 128 s + 8 e + m with s of 0 or 1, e from 5 to 8 and m from 0 to 7.
All inputs are finite; a program needn't handle non-finite values.
Results may differ from the reference program's by a relative error of at most 0.015.
Values may be sent and summed in bfloat16 or wider, within the bound.
No kernel may reach another device: no remote copies, remote signals or barrier semaphores. Data moves between devices by JAX's collectives and lax.ppermute only.
A program may use at most 128 MiB of HBM per device.

```python
import math
import jax
import jax.numpy as jnp
from jax import lax

D = 2048
HEADS = 16
HEAD_DIM = 128
STRETCH = 64
BLOCK = 128
HD = 2048
TOKENS = 65536
LEVELS = 11
N_MP = 8


def draw_w_proj(key, part):
    first, second = jax.random.split(jax.random.fold_in(key, 11), 2)
    width = HEADS * HEAD_DIM
    column_scale = jnp.exp(jax.random.uniform(first, (1, 4, width), jnp.float32, math.log(0.3), math.log(3.0)))
    base = jax.random.normal(second, (D, 4, width), jnp.float32)
    return (base * column_scale / math.sqrt(D)).astype(jnp.bfloat16)


def draw_w_codes(key, part):
    first, second, third = jax.random.split(jax.random.fold_in(key, 23), 3)
    width = HEADS * HEAD_DIM
    negative = jax.random.randint(first, (width, D), 0, 2, jnp.int32)
    exponent = jax.random.randint(second, (width, D), 5, 9, jnp.int32)
    mantissa = jax.random.randint(third, (width, D), 0, 8, jnp.int32)
    return 128 * negative + 8 * exponent + mantissa


def plant(values, rng, least, high):
    longest = values.shape.index(max(values.shape))
    spots = []
    for shift in (0, 1):
        where = [jax.random.randint(jax.random.fold_in(rng, axis), (), 0, length) for axis, length in enumerate(values.shape)]
        where[longest] = (where[longest] + shift) % values.shape[longest]
        spots.append(tuple(where))
    return values.at[spots[0]].set(least).at[spots[1]].set(high)


def block_scale(key, dims, cuts, smallest, largest):
    loudness = 1.0
    for axis_at, blocks in cuts:
        draws = jax.random.uniform(jax.random.fold_in(jax.random.fold_in(key, 6), axis_at), (blocks,), jnp.float32, smallest / len(cuts), largest / len(cuts))
        loudness = loudness * jnp.repeat(jnp.exp(draws), dims[axis_at] // blocks).reshape((-1,) + (1,) * (len(dims) - 1 - axis_at))
    return loudness


def gaussian(rng, extent, spread, bound, cuts=(), dtype=jnp.bfloat16):
    level = block_scale(rng, extent, cuts, -0.22, 0.18) if cuts else 1.0
    entries = jax.random.normal(rng, extent, jnp.float32) * spread * level
    return jnp.minimum(jnp.maximum(entries, -bound), bound).astype(dtype)


def setup_inputs(seed: int = 0) -> dict:
    key_list = jax.random.split(jax.random.key(seed), 7)
    tokens = gaussian(key_list[0], (TOKENS, D), 1.0, 6.0, ((0, 32),))
    w_proj = draw_w_proj(jax.random.fold_in(key_list[6], 71), 0)
    gain = jnp.clip(1.0 + 0.15 * jax.random.normal(key_list[2], (HD,), jnp.float32), 0.25, 1.75)
    level_codes = plant(jax.random.randint(key_list[3], (LEVELS, HEADS, TOKENS), 0, 256), jax.random.fold_in(key_list[3], 1), 0, 255).astype(jnp.int32)
    w_codes = draw_w_codes(jax.random.fold_in(key_list[6], 71), 0)
    block_exponent = plant(jax.random.randint(key_list[5], (HD // BLOCK, D // BLOCK), -7, -4), jax.random.fold_in(key_list[5], 1), -7, (-4) - 1).astype(jnp.int32)
    return dict(tokens=tokens, w_proj=w_proj, gain=gain, level_codes=level_codes, w_codes=w_codes, block_exponent=block_exponent)


def power_of_two(field, bits):
    result = jnp.ones(field.shape, jnp.float32)
    for bit in range(bits):
        result = result * jnp.where(field // 2 ** bit % 2 == 1, jnp.float32(2.0 ** 2 ** bit), jnp.float32(1.0))
    return result

def decode_weight(codes, exponents, block):
    negative = codes // 128
    exponent = codes // 8 % 16
    mantissa = codes % 8
    magnitude = (8 + mantissa).astype(jnp.float32) * (1 - 2 * negative).astype(jnp.float32)
    magnitude = magnitude * power_of_two(exponent, 4) * jnp.float32(2.0 ** (-10))
    scales = power_of_two(exponents + 16, 5) * jnp.float32(2.0 ** (-16))
    rows, columns = codes.shape
    shaped = magnitude.reshape(rows // block, block, columns // block, block) * scales[:, None, :, None]
    return shaped.reshape(rows, columns).astype(jnp.bfloat16)

def head_mix(inputs):
    query, keys, values, level_weight = inputs
    stretches = TOKENS // STRETCH
    query_blocks = query.reshape(stretches, STRETCH, HEAD_DIM)
    key_blocks = keys.reshape(stretches, STRETCH, HEAD_DIM).astype(jnp.float32)
    value_blocks = values.reshape(stretches, STRETCH, HEAD_DIM).astype(jnp.float32)
    scores = jnp.einsum('ntd,nsd->nts', query_blocks.astype(jnp.float32), key_blocks)
    causal = jnp.tril(jnp.ones((STRETCH, STRETCH), bool))
    weights = (jnp.where(causal[None], scores, 0.0) * (1.0 / math.sqrt(HEAD_DIM * STRETCH))).astype(jnp.bfloat16)
    local = jnp.einsum('nts,nsd->ntd', weights.astype(jnp.float32), value_blocks)
    total = level_weight[0].reshape(stretches, STRETCH)[:, :, None] * local
    blocks = jnp.einsum('ntd,nte->nde', key_blocks, value_blocks)
    for level in range(LEVELS - 1):
        count = stretches >> level + 1
        span = STRETCH << level
        pairs = blocks.reshape(count, 2, HEAD_DIM, HEAD_DIM)
        sibling = pairs[:, 0].astype(jnp.bfloat16)
        second = query_blocks.reshape(count, 2, span, HEAD_DIM)[:, 1]
        term = jnp.einsum('ptd,pde->pte', second.astype(jnp.float32), sibling.astype(jnp.float32))
        term = term * (1.0 / math.sqrt(HEAD_DIM * span))
        weight_second = level_weight[level + 1].reshape(count, 2, span)[:, 1]
        placed = jnp.stack([jnp.zeros_like(term), weight_second[:, :, None] * term], 1)
        total = total + placed.reshape(stretches, STRETCH, HEAD_DIM)
        blocks = pairs[:, 0] + pairs[:, 1]
    return total.reshape(TOKENS, HEAD_DIM)

def reference(tokens, w_proj, gain, level_codes, w_codes, block_exponent):
    width = HEADS * HEAD_DIM
    projected = jnp.dot(tokens, w_proj.reshape(D, 4 * width), preferred_element_type=jnp.float32)
    projected = projected.reshape(TOKENS, 4, HEADS, HEAD_DIM)
    query = projected[:, 0].astype(jnp.bfloat16).transpose(1, 0, 2)
    keys = projected[:, 1].astype(jnp.bfloat16).transpose(1, 0, 2)
    values = projected[:, 2].astype(jnp.bfloat16).transpose(1, 0, 2)
    gate = jax.nn.silu(projected[:, 3].reshape(TOKENS, width))
    level_weight = (level_codes.astype(jnp.float32) / 128.0).transpose(1, 0, 2)
    memory = lax.map(head_mix, (query, keys, values, level_weight)).transpose(1, 0, 2)
    normed = memory * lax.rsqrt(lax.optimization_barrier(jnp.mean(memory * memory, axis=-1, keepdims=True)) + 1e-06)
    attended = (normed.reshape(TOKENS, width) * gain * gate).astype(jnp.bfloat16)
    weight = decode_weight(w_codes, block_exponent, BLOCK)
    group = width // N_MP
    mixed = jnp.zeros((TOKENS, D), jnp.float32)
    for member in range(N_MP):
        partial_value = jnp.dot(attended[:, member * group:(member + 1) * group], weight[member * group:(member + 1) * group], preferred_element_type=jnp.float32).astype(jnp.bfloat16)
        partial_value = lax.optimization_barrier(partial_value)
        mixed = mixed + partial_value.astype(jnp.float32)
    return mixed.astype(jnp.bfloat16)
```

```python
import math

import jax
import jax.numpy as jnp
from jax import lax
from jax.experimental import pallas as pl
from jax.experimental.pallas import tpu as pltpu
from jax.sharding import PartitionSpec as P

D = 2048
HEAD_DIM = 128
STRETCH = 64
BLOCK = 128
TILE = 256
F32 = jnp.float32
BF16 = jnp.bfloat16
VMEM_LIMIT = 56 * 1024 * 1024


def cost(flops, size):
    return pl.CostEstimate(flops=int(flops), bytes_accessed=int(size), transcendentals=0)


def full(shape):
    zeros = (0,) * len(shape)
    return pl.BlockSpec(shape, lambda *_: zeros)


def dot(a, b):
    return jnp.dot(a, b, preferred_element_type=F32)


def dot_nt(a, b):
    return lax.dot_general(a, b, (((1,), (1,)), ((), ())), preferred_element_type=F32)


def power_of_two(field, bits):
    result = jnp.ones(field.shape, F32)
    for bit in range(bits):
        result = result * jnp.where(
            (field >> bit) & 1 == 1, jnp.float32(2.0**2**bit), jnp.float32(1.0)
        )
    return result


def decode_weight(codes, exponents, block):
    negative = codes >> 7
    exponent = (codes >> 3) & 15
    mantissa = codes & 7
    magnitude = (8 + mantissa).astype(F32) * (1 - 2 * negative).astype(F32)
    magnitude = magnitude * power_of_two(exponent, 4) * jnp.float32(2.0 ** (-10))
    scales = power_of_two(exponents + 16, 5) * jnp.float32(2.0 ** (-16))
    rows, columns = codes.shape
    shaped = (
        magnitude.reshape(rows // block, block, columns // block, block) * scales[:, None, :, None]
    )
    return shaped.reshape(rows, columns).astype(BF16)


def unpack_parts(r_ref, w_ref, f_ref, parts):
    chunk = f_ref.shape[1]
    for step in range(r_ref.shape[0] // chunk):
        slot = step % 2
        f_ref[slot] = r_ref[pl.ds(step * chunk, chunk), :].astype(F32)
        rows = chunk // 8
        for at, part in enumerate(parts):
            for half in range(2):
                piece = f_ref[slot, pl.ds(half * 4 + part, rows, stride=8), :]
                w_ref[pl.ds(step * rows, rows), pl.ds(at * 256 + half * 128, 128)] = piece.astype(BF16)


def keys_values_kernel(r_ref, x_ref, k_ref, vt_ref, sr_ref, tot_ref, w_ref, f_ref, u_ref):
    step = pl.program_id(0)

    @pl.when(step == 0)
    def _():
        unpack_parts(r_ref, w_ref, f_ref, (1, 2))

    projected = dot(x_ref[...], w_ref[...])
    keys = projected[:, :256].astype(BF16)
    k_ref[...] = keys
    vt = projected[:, 256:].T.astype(BF16)
    vt_ref[...] = vt
    subs = x_ref.shape[0] // TILE
    for sub in range(subs):
        at = slice(sub * TILE, (sub + 1) * TILE)
        u = dot(vt[:, at], keys[at])
        for head in range(2):
            lanes = slice(head * 128, (head + 1) * 128)
            u_ref[step * subs + sub, head] = u[lanes, lanes]

    @pl.when(step == pl.num_programs(0) - 1)
    def _():
        u01 = u_ref[0] + u_ref[1]
        u03 = u01 + (u_ref[2] + u_ref[3])
        u45 = u_ref[4] + u_ref[5]
        for at, tile in enumerate((0, 2, 4, 6)):
            sr_ref[at] = u_ref[tile].astype(BF16)
        sr_ref[4] = u01.astype(BF16)
        sr_ref[5] = u45.astype(BF16)
        sr_ref[6] = u03.astype(BF16)
        tot_ref[...] = (u03 + (u45 + (u_ref[6] + u_ref[7]))).astype(BF16)


def keys_values(r, tokens):
    rows = tokens.shape[0]
    tile = 512
    return pl.pallas_call(
        keys_values_kernel,
        grid=(rows // tile,),
        in_specs=[full(r.shape), pl.BlockSpec((tile, D), lambda i: (i, 0))],
        out_specs=[
            pl.BlockSpec((tile, 256), lambda i: (i, 0)),
            pl.BlockSpec((256, tile), lambda i: (0, i)),
            full((7, 2, 128, 128)),
            full((2, 128, 128)),
        ],
        out_shape=[
            jax.ShapeDtypeStruct((rows, 256), BF16),
            jax.ShapeDtypeStruct((256, rows), BF16),
            jax.ShapeDtypeStruct((7, 2, 128, 128), BF16),
            jax.ShapeDtypeStruct((2, 128, 128), BF16),
        ],
        scratch_shapes=[
            pltpu.VMEM((D, 512), BF16),
            pltpu.VMEM((2, 2048, 128), F32),
            pltpu.VMEM((8, 2, 128, 128), F32),
        ],
        compiler_params=pltpu.CompilerParams(vmem_limit_bytes=VMEM_LIMIT),
        cost_estimate=cost(2 * rows * D * 512, 14 * 2**20),
        name="keys_values",
    )(r, tokens)


def query_gate_kernel(r_ref, gain_ref, x_ref, q_ref, gg_ref, w_ref, f_ref):
    @pl.when(pl.program_id(0) == 0)
    def _():
        unpack_parts(r_ref, w_ref, f_ref, (0, 3))

    projected = dot(x_ref[...], w_ref[...])
    q_ref[...] = projected[:, :256].astype(BF16)
    g = projected[:, 256:]
    gg_ref[...] = gain_ref[...] * (g / (1.0 + jnp.exp(-g)))


def query_gate(r, gain, tokens):
    rows = tokens.shape[0]
    tile = 512
    return pl.pallas_call(
        query_gate_kernel,
        grid=(rows // tile,),
        in_specs=[full(r.shape), full((1, 256)), pl.BlockSpec((tile, D), lambda i: (i, 0))],
        out_specs=[
            pl.BlockSpec((tile, 256), lambda i: (i, 0)),
            pl.BlockSpec((tile, 256), lambda i: (i, 0)),
        ],
        out_shape=[
            jax.ShapeDtypeStruct((rows, 256), BF16),
            jax.ShapeDtypeStruct((rows, 256), F32),
        ],
        scratch_shapes=[pltpu.VMEM((D, 512), BF16), pltpu.VMEM((2, 2048, 128), F32)],
        compiler_params=pltpu.CompilerParams(vmem_limit_bytes=VMEM_LIMIT),
        cost_estimate=cost(2 * rows * D * 512, 15 * 2**20),
        name="query_gate",
    )(r, gain, tokens)


def level_scale(span):
    return 1.0 / (128.0 * math.sqrt(HEAD_DIM * span))


def local_kernel(q_ref, k_ref, vt_ref, codes_ref, sr_ref, out_ref):
    step = pl.program_id(0)
    subs = q_ref.shape[0] // TILE
    s = lax.broadcasted_iota(jnp.int32, (TILE, TILE), 0)
    t = lax.broadcasted_iota(jnp.int32, (TILE, TILE), 1)
    gap = (t >> 6) - (s >> 6)
    inside = (gap == 0) & (s <= t)
    odd = (gap == 1) & ((t >> 6) & 1 == 1)
    second = ((t >> 7) - (s >> 7) == 1)
    for sub in range(subs):
        tile = step * subs + sub
        at = slice(sub * TILE, (sub + 1) * TILE)
        flags = [((tile >> bit) & 1).astype(F32) for bit in range(3)]
        reads = (tile >> 1, 4 + (tile >> 2), 6)
        for head in range(2):
            lanes = slice(head * 128, (head + 1) * 128)

            def row(level, span, head=head, at=at):
                return codes_ref[level, head : head + 1, at].astype(F32) * level_scale(span)

            left = jnp.concatenate([k_ref[at, lanes]] + [sr_ref[r, head] for r in reads], axis=0)
            product = dot_nt(left, q_ref[at, lanes])
            weight = jnp.where(
                inside,
                row(0, STRETCH),
                jnp.where(
                    odd, row(1, STRETCH), jnp.where(second, row(2, 2 * STRETCH), 0.0)
                ),
            )
            masked = (product[:TILE] * weight).astype(BF16)
            total = dot(vt_ref[lanes, at], masked)
            for j in range(3):
                total += (row(3 + j, TILE << j) * flags[j]) * product[TILE + j * 128 : TILE + (j + 1) * 128]
            out_ref[lanes, at] = total


def local_levels(query, keys, vt, codes, sr):
    rows = query.shape[0]
    tile = 512
    return pl.pallas_call(
        local_kernel,
        grid=(rows // tile,),
        in_specs=[
            pl.BlockSpec((tile, 256), lambda i: (i, 0)),
            pl.BlockSpec((tile, 256), lambda i: (i, 0)),
            pl.BlockSpec((256, tile), lambda i: (0, i)),
            pl.BlockSpec((11, 2, tile), lambda i: (0, 0, i)),
            full(sr.shape),
        ],
        out_specs=pl.BlockSpec((256, tile), lambda i: (0, i)),
        out_shape=jax.ShapeDtypeStruct((256, rows), F32),
        compiler_params=pltpu.CompilerParams(vmem_limit_bytes=VMEM_LIMIT),
        cost_estimate=cost(6e9, 6 * 2**20),
        name="local_levels",
    )(query, keys, vt, codes, sr)


def attend_kernel(rows_here, flags_ref, q_ref, m_ref, gg_ref, codes_ref, r1, r2, r3, g1, g2, g3, h1, out_ref, sd_ref):
    @pl.when(pl.program_id(0) == 0)
    def _():
        for head in range(2):
            sd_ref[head, pl.ds(0, 128), :] = r1[head]
            sd_ref[head, pl.ds(128, 128), :] = (r2[head].astype(F32) + r3[head].astype(F32)).astype(BF16)
            sd_ref[head, pl.ds(256, 128), :] = g1[head]
            sd_ref[head, pl.ds(384, 128), :] = (g2[head].astype(F32) + g3[head].astype(F32)).astype(BF16)
            sd_ref[head, pl.ds(512, 128), :] = h1[head]

    for head in range(2):
        lanes = slice(head * 128, (head + 1) * 128)
        product = dot_nt(sd_ref[head], q_ref[:, lanes])
        memory = m_ref[lanes, :]
        for j in range(5):
            scale = flags_ref[j] * level_scale(rows_here << j)
            row = codes_ref[6 + j, head : head + 1, :].astype(F32) * scale
            memory += row * product[j * 128 : (j + 1) * 128]
        mean = jnp.mean(memory * memory, axis=0, keepdims=True)
        normed = memory * lax.rsqrt(mean + 1e-06)
        out_ref[:, lanes] = (normed.T * gg_ref[:, lanes]).astype(BF16)


def attend(flags, query, local, gg, codes, reads):
    rows = query.shape[0]
    tile = 512
    return pl.pallas_call(
        lambda *refs: attend_kernel(rows, *refs),
        grid=(rows // tile,),
        in_specs=[
            pl.BlockSpec(memory_space=pltpu.SMEM),
            pl.BlockSpec((tile, 256), lambda i: (i, 0)),
            pl.BlockSpec((256, tile), lambda i: (0, i)),
            pl.BlockSpec((tile, 256), lambda i: (i, 0)),
            pl.BlockSpec((11, 2, tile), lambda i: (0, 0, i)),
        ]
        + [full((2, 128, 128))] * 7,
        out_specs=pl.BlockSpec((tile, 256), lambda i: (i, 0)),
        out_shape=jax.ShapeDtypeStruct((rows, 256), BF16),
        scratch_shapes=[pltpu.VMEM((2, 640, 128), BF16)],
        compiler_params=pltpu.CompilerParams(vmem_limit_bytes=VMEM_LIMIT),
        cost_estimate=cost(3e9, 6 * 2**20),
        name="attend",
    )(flags, query, local, gg, codes, *reads)


def project_kernel(at_ref, a_ref, *refs):
    out_ref = refs[-1]
    total = None
    for place, (first, w_ref) in enumerate(zip((0, 0, 0, 0, 128) * 2, refs[:-1], strict=True)):
        block = a_ref[at_ref[place]]
        width = w_ref.shape[0]
        term = dot(block[:, first : first + width], w_ref[...])
        total = term if total is None else total + term
    out_ref[...] = total.astype(BF16)


def project(places, attended, pieces):
    columns = 512
    return pl.pallas_call(
        project_kernel,
        grid=(D // columns,),
        in_specs=[pl.BlockSpec(memory_space=pltpu.SMEM), full(attended.shape)]
        + [pl.BlockSpec((p.shape[0], columns), lambda i: (0, i)) for p in pieces],
        out_specs=pl.BlockSpec((attended.shape[1], columns), lambda i: (0, i)),
        out_shape=jax.ShapeDtypeStruct((attended.shape[1], D), BF16),
        compiler_params=pltpu.CompilerParams(vmem_limit_bytes=VMEM_LIMIT),
        cost_estimate=cost(2 * 256 * 2048 * 2048, 10 * 2**20),
        name="project",
    )(places, attended, *pieces)


def body(tokens, w_proj, gain, level_codes, w_codes, block_exponent):
    place = lax.axis_index("mp")
    position = lax.axis_index("seq")

    def along_x(block, by):
        return lax.ppermute(block, "mp", [(m, (m // 2 + by) % 4 * 2 + m % 2) for m in range(8)])

    def other_core(block):
        return lax.ppermute(block, "mp", [(m, m ^ 1) for m in range(8)])

    weight = decode_weight(w_codes, block_exponent, BLOCK)
    from_left = along_x(weight, 1)
    from_right = along_x(weight, -1)
    far_top = along_x(from_left[:128], 1)
    far_low = along_x(from_right[128:], -1)
    pieces = [weight, from_left, from_right, far_top, far_low]
    pieces = pieces + [other_core(piece) for piece in pieces]
    x, core = place // 2, place % 2
    ways = jnp.stack([x, (x + 3) % 4, (x + 1) % 4, (x + 2) % 4, (x + 2) % 4])
    places = jnp.concatenate([ways * 2 + core, ways * 2 + 1 - core]).astype(jnp.int32)

    r = w_proj.reshape(D, 4, 2, 128).transpose(0, 2, 1, 3).reshape(D * 8, 128)
    keys, vt, sr, state = keys_values(r, tokens)

    def across(block, pairs):
        return lax.ppermute(block, "seq", pairs)

    r1, r2, r3 = [across(state, [(i, i ^ k) for i in range(32)]) for k in (1, 2, 3)]
    group = state.astype(F32) + r1.astype(F32) + (r2.astype(F32) + r3.astype(F32))
    sent = group.astype(BF16)
    g1, g2, g3 = [across(sent, [(i, i ^ (4 * k)) for i in range(32)]) for k in (1, 2, 3)]
    half = group + g1.astype(F32) + (g2.astype(F32) + g3.astype(F32))
    h1 = across(half.astype(BF16), [(i, i + 16) for i in range(16)])
    flags = (position >> jnp.arange(5, dtype=jnp.int32) & 1).astype(F32)

    query, gg = query_gate(r, gain.reshape(1, 256), tokens)
    local = local_levels(query, keys, vt, level_codes, sr)
    attended = attend(flags, query, local, gg, level_codes, (r1, r2, r3, g1, g2, g3, h1))
    attended = lax.all_to_all(attended.reshape(8, 256, 256), "mp", 0, 0, tiled=True)
    return project(places, attended, pieces)


def solution(mesh):
    placed = (
        P("seq", None),
        P(None, None, "mp"),
        P("mp"),
        P(None, "mp", "seq"),
        P("mp", None),
        P("mp", None),
    )
    return jax.shard_map(
        body, mesh=mesh, in_specs=placed, out_specs=P(("seq", "mp"), None), check_vma=False
    )
```

```python
import math

import jax
import jax.numpy as jnp
from jax import lax
from jax.experimental import pallas as pl
from jax.experimental.pallas import tpu as pltpu
from jax.sharding import PartitionSpec as P

D = 2048
HEAD_DIM = 128
STRETCH = 64
BLOCK = 128
TILE = 256
F32 = jnp.float32
BF16 = jnp.bfloat16
MIB = 1024 * 1024
VMEM_LIMIT = 60 * MIB


def cost(flops, size):
    return pl.CostEstimate(flops=int(flops), bytes_accessed=int(size), transcendentals=0)


def full(shape, buffers=2):
    zeros = (0,) * len(shape)
    return pl.BlockSpec(shape, lambda *_: zeros, pipeline_mode=pl.Buffered(buffers))


def dot(a, b):
    return jnp.dot(a, b, preferred_element_type=F32)


def dot_nt(a, b):
    return lax.dot_general(a, b, (((1,), (1,)), ((), ())), preferred_element_type=F32)


def decode_kernel(exponent_ref, codes_ref, out_ref):
    step = pl.program_id(0)
    blocks = codes_ref.shape[1] // BLOCK
    for half in range(2):
        rows = slice(half * BLOCK, (half + 1) * BLOCK)
        for block in range(blocks):
            lanes = slice(block * BLOCK, (block + 1) * BLOCK)
            codes = codes_ref[rows, lanes]
            power = exponent_ref[half, step * blocks + block] + 16
            scale = jnp.left_shift(jnp.int32(1), power).astype(F32) * jnp.float32(2.0 ** (-26))
            size = jnp.left_shift(8 + (codes & 7), (codes >> 3) & 15)
            size = jnp.where(codes >= 128, -size, size).astype(F32)
            out_ref[rows, lanes] = (size * scale).astype(BF16)


def decode_weight(codes, exponents):
    columns = 1024
    return pl.pallas_call(
        decode_kernel,
        grid=(D // columns,),
        in_specs=[
            pl.BlockSpec(memory_space=pltpu.SMEM),
            pl.BlockSpec((2 * BLOCK, columns), lambda i: (0, i)),
        ],
        out_specs=pl.BlockSpec((2 * BLOCK, columns), lambda i: (0, i)),
        out_shape=jax.ShapeDtypeStruct((2 * BLOCK, D), BF16),
        compiler_params=pltpu.CompilerParams(vmem_limit_bytes=VMEM_LIMIT),
        cost_estimate=cost(8e6, 3 * MIB),
        name="decode_weight",
    )(exponents, codes)


CHUNKS = 8
ROWS = 512
PARTS = (1, 2, 0, 3)


def unpack_chunk(chunk, parts, r_buf, w_ref, f_ref):
    size = r_buf.shape[0] // CHUNKS
    slot = chunk % f_ref.shape[0]
    f_ref[slot] = r_buf[pl.ds(chunk * size, size), :].astype(F32)
    rows = size // 8
    for at, part in enumerate(parts):
        for half in range(2):
            piece = f_ref[slot, pl.ds(half * 4 + part, rows, stride=8), :]
            w_ref[pl.ds(chunk * rows, rows), pl.ds(at * 256 + half * 128, 128)] = piece.astype(BF16)


def project_tiles(r_hbm, x_hbm, r_buf, x_buf, w_ref, f_ref, acc_ref, r_sem, x_sem, finish):
    size = r_buf.shape[0] // CHUNKS
    deep = w_ref.shape[0] // CHUNKS
    tiles = x_buf.shape[0] // ROWS

    def chunk_copy(chunk):
        at = pl.ds(chunk * size, size)
        return pltpu.make_async_copy(r_hbm.at[at], r_buf.at[at], r_sem.at[chunk])

    def tile_copy(tile):
        at = pl.ds(tile * ROWS, ROWS)
        return pltpu.make_async_copy(x_hbm.at[at], x_buf.at[at], x_sem.at[tile])

    r_copies = [chunk_copy(chunk) for chunk in range(CHUNKS)]
    x_copies = [tile_copy(tile) for tile in range(tiles)]
    for copy in r_copies[:2] + x_copies[:1] + r_copies[2:] + x_copies[1:]:
        copy.start()
    for chunk in range(2):
        r_copies[chunk].wait()
        unpack_chunk(chunk, PARTS, r_buf, w_ref, f_ref)
    x_copies[0].wait()
    for chunk in range(CHUNKS):
        if chunk + 2 < CHUNKS:
            r_copies[chunk + 2].wait()
        at = pl.ds(chunk * deep, deep)
        term = dot(x_buf[pl.ds(0, ROWS), at], w_ref[at, :])
        if chunk == 0:
            acc_ref[0] = term
        else:
            acc_ref[0] += term
        if chunk + 2 < CHUNKS:
            unpack_chunk(chunk + 2, PARTS, r_buf, w_ref, f_ref)
    for tile in range(1, tiles):
        x_copies[tile].wait()
        acc_ref[tile % 2] = dot(x_buf[pl.ds(tile * ROWS, ROWS), :], w_ref[...])
        finish(tile - 1)
    finish(tiles - 1)


def projection_scratch(rows):
    return [
        pltpu.VMEM((D * 8, 128), BF16),
        pltpu.VMEM((rows, D), BF16),
        pltpu.VMEM((D, 1024), BF16),
        pltpu.VMEM((2, D * 8 // CHUNKS, 128), F32),
        pltpu.VMEM((2, ROWS, 1024), F32),
        pltpu.SemaphoreType.DMA((CHUNKS,)),
        pltpu.SemaphoreType.DMA((rows // ROWS,)),
    ]


def projections_kernel(r_hbm, gain_ref, x_hbm, k_hbm, vt_hbm, q_hbm, gg_hbm, sr_ref, tot_ref, *scratch):
    *shared, k_buf, vt_buf, q_buf, gg_buf, u_ref, out_sem = scratch
    acc_ref = shared[4]
    copies = []

    def finish(tile):
        rows = pl.ds(tile * ROWS, ROWS)
        keys = acc_ref[tile % 2, :, 0:256].astype(BF16)
        k_buf[rows, :] = keys
        vt = acc_ref[tile % 2, :, 256:512].T.astype(BF16)
        vt_buf[:, rows] = vt
        q_buf[rows, :] = acc_ref[tile % 2, :, 512:768].astype(BF16)
        g = acc_ref[tile % 2, :, 768:1024]
        gg_buf[rows, :] = (gain_ref[...] * (g / (1.0 + jnp.exp(-g)))).astype(BF16)
        for place, (source, target) in enumerate(
            (
                (k_buf.at[rows], k_hbm.at[rows]),
                (vt_buf.at[:, rows], vt_hbm.at[:, rows]),
                (q_buf.at[rows], q_hbm.at[rows]),
                (gg_buf.at[rows], gg_hbm.at[rows]),
            )
        ):
            copy = pltpu.make_async_copy(source, target, out_sem.at[tile, place])
            copy.start()
            copies.append(copy)
        for sub in range(ROWS // TILE):
            at = slice(sub * TILE, (sub + 1) * TILE)
            u = dot(vt[:, at], keys[at])
            for head in range(2):
                lanes = slice(head * 128, (head + 1) * 128)
                u_ref[tile * (ROWS // TILE) + sub, head] = u[lanes, lanes]

    project_tiles(r_hbm, x_hbm, *shared, finish)
    u01 = u_ref[0] + u_ref[1]
    u03 = u01 + (u_ref[2] + u_ref[3])
    u45 = u_ref[4] + u_ref[5]
    for at, tile in enumerate((0, 2, 4, 6)):
        sr_ref[at] = u_ref[tile].astype(BF16)
    sr_ref[4] = u01.astype(BF16)
    sr_ref[5] = u45.astype(BF16)
    sr_ref[6] = u03.astype(BF16)
    tot_ref[...] = (u03 + (u45 + (u_ref[6] + u_ref[7]))).astype(BF16)
    for copy in copies:
        copy.wait()


def projections(r, gain, tokens):
    rows = tokens.shape[0]
    anywhere = pl.BlockSpec(memory_space=pl.ANY)
    return pl.pallas_call(
        projections_kernel,
        grid=(1,),
        in_specs=[anywhere, full((1, 256), 1), anywhere],
        out_specs=[anywhere] * 4 + [full((7, 2, 128, 128), 1), full((2, 128, 128), 1)],
        out_shape=[
            jax.ShapeDtypeStruct((rows, 256), BF16),
            jax.ShapeDtypeStruct((256, rows), BF16),
            jax.ShapeDtypeStruct((rows, 256), BF16),
            jax.ShapeDtypeStruct((rows, 256), BF16),
            jax.ShapeDtypeStruct((7, 2, 128, 128), BF16),
            jax.ShapeDtypeStruct((2, 128, 128), BF16),
        ],
        scratch_shapes=projection_scratch(rows)
        + [
            pltpu.VMEM((rows, 256), BF16),
            pltpu.VMEM((256, rows), BF16),
            pltpu.VMEM((rows, 256), BF16),
            pltpu.VMEM((rows, 256), BF16),
            pltpu.VMEM((8, 2, 128, 128), F32),
            pltpu.SemaphoreType.DMA((rows // ROWS, 4)),
        ],
        compiler_params=pltpu.CompilerParams(vmem_limit_bytes=VMEM_LIMIT),
        cost_estimate=cost(2 * rows * D * 1024, 18 * MIB),
        name="projections",
    )(r, gain, tokens)


def level_scale(span):
    return 1.0 / (128.0 * math.sqrt(HEAD_DIM * span))


def local_kernel(start, q_ref, k_ref, vt_ref, codes_ref, sr_ref, *rest):
    out_ref = rest[-1]
    subs = q_ref.shape[0] // TILE
    s = lax.broadcasted_iota(jnp.int32, (TILE, TILE), 0)
    t = lax.broadcasted_iota(jnp.int32, (TILE, TILE), 1)
    gap = (t >> 6) - (s >> 6)
    inside = (gap == 0) & (s <= t)
    odd = (gap == 1) & ((t >> 6) & 1 == 1)
    second = ((t >> 7) - (s >> 7) == 1)
    for sub in range(subs):
        tile = start + sub
        at = slice(sub * TILE, (sub + 1) * TILE)
        flags = [float((tile >> bit) & 1) for bit in range(3)]
        reads = (tile >> 1, 4 + (tile >> 2), 6)
        for head in range(2):
            lanes = slice(head * 128, (head + 1) * 128)

            def row(level, span, head=head, at=at):
                return codes_ref[level, head : head + 1, at].astype(F32) * level_scale(span)

            left = jnp.concatenate(
                [k_ref[at, lanes]] + [sr_ref[r, head] for r, flag in zip(reads, flags) if flag], axis=0
            )
            product = dot_nt(left, q_ref[at, lanes])
            weight = jnp.where(
                inside,
                row(0, STRETCH),
                jnp.where(
                    odd, row(1, STRETCH), jnp.where(second, row(2, 2 * STRETCH), 0.0)
                ),
            )
            masked = (product[:TILE] * weight).astype(BF16)
            total = dot(vt_ref[lanes, at], masked)
            levels = [j for j in range(3) if flags[j]]
            for place, j in enumerate(levels):
                rows = slice(TILE + place * 128, TILE + (place + 1) * 128)
                total += row(3 + j, TILE << j) * product[rows]
            out_ref[lanes, at] = total.astype(BF16)


def local_levels(part, query, keys, vt, codes, sr, *earlier):
    rows = query.shape[0]
    return pl.pallas_call(
        lambda *refs: local_kernel(part * (ROWS // TILE), *refs),
        grid=(1,),
        in_specs=[
            pl.BlockSpec((ROWS, 256), lambda i: (part, 0), pipeline_mode=pl.Buffered(1)),
            pl.BlockSpec((ROWS, 256), lambda i: (part, 0), pipeline_mode=pl.Buffered(1)),
            pl.BlockSpec((256, ROWS), lambda i: (0, part), pipeline_mode=pl.Buffered(1)),
            pl.BlockSpec((11, 2, ROWS), lambda i: (0, 0, part), pipeline_mode=pl.Buffered(1)),
            full(sr.shape, 1),
        ]
        + [pl.BlockSpec(memory_space=pl.ANY)] * len(earlier),
        out_specs=pl.BlockSpec((256, ROWS), lambda i: (0, part), pipeline_mode=pl.Buffered(1)),
        out_shape=jax.ShapeDtypeStruct((256, rows), BF16),
        input_output_aliases={5: 0} if earlier else {},
        compiler_params=pltpu.CompilerParams(vmem_limit_bytes=VMEM_LIMIT),
        cost_estimate=cost(3e9, 2 * MIB),
        name=f"local_levels_{part}",
    )(query, keys, vt, codes, sr, *earlier)


def attend_kernel(rows_here, at_ref, q_ref, m_ref, gg_ref, codes_ref, *refs):
    *read_refs, out_ref, sd_ref = refs
    position = at_ref[0]

    @pl.when(pl.program_id(0) == 0)
    def _():
        for j, read_ref in enumerate(read_refs):
            for head in range(2):
                sd_ref[head, pl.ds(j * 128, 128), :] = read_ref[head]

    for head in range(2):
        lanes = slice(head * 128, (head + 1) * 128)
        product = dot_nt(sd_ref[head], q_ref[:, lanes])
        memory = m_ref[lanes, :].astype(F32)
        for j in range(5):
            scale = ((position >> j) & 1).astype(F32) * level_scale(rows_here << j)
            row = codes_ref[6 + j, head : head + 1, :].astype(F32) * scale
            memory += row * product[j * 128 : (j + 1) * 128]
        mean = jnp.mean(memory * memory, axis=0, keepdims=True)
        normed = memory * lax.rsqrt(mean + 1e-06)
        out_ref[:, lanes] = (normed.T * gg_ref[:, lanes].astype(F32)).astype(BF16)


def attend(position, query, local, gg, codes, reads):
    rows = query.shape[0]
    tile = 512
    return pl.pallas_call(
        lambda *refs: attend_kernel(rows, *refs),
        grid=(rows // tile,),
        in_specs=[
            pl.BlockSpec(memory_space=pltpu.SMEM),
            pl.BlockSpec((tile, 256), lambda i: (i, 0)),
            pl.BlockSpec((256, tile), lambda i: (0, i)),
            pl.BlockSpec((tile, 256), lambda i: (i, 0)),
            pl.BlockSpec((11, 2, tile), lambda i: (0, 0, i)),
        ]
        + [full(read.shape, 1) for read in reads],
        out_specs=pl.BlockSpec((tile, 256), lambda i: (i, 0)),
        out_shape=jax.ShapeDtypeStruct((rows, 256), BF16),
        scratch_shapes=[pltpu.VMEM((2, 640, 128), BF16)],
        compiler_params=pltpu.CompilerParams(vmem_limit_bytes=VMEM_LIMIT),
        cost_estimate=cost(3e9, 6 * MIB),
        name="attend",
    )(position, query, local, gg, codes, *reads)


def project_kernel(at_ref, a_ref, *refs):
    pieces, (out_ref, buf, acc_ref, sem) = refs[:-4], refs[-4:]
    x, core = at_ref[0] >> 1, at_ref[0] & 1
    copies = [pltpu.make_async_copy(piece, buf.at[p], sem.at[p]) for p, piece in enumerate(pieces)]
    for copy in copies:
        copy.start()
    half = len(pieces) // 2
    for p in range(half):
        blocks, weights = [], []
        for flip in range(2):
            copies[p + flip * half].wait()
            blocks.append(a_ref[((x + (0, 3, 1, 2)[p]) & 3) * 2 + (core ^ flip)])
            weights.append(buf[p + flip * half])
        term = dot(jnp.concatenate(blocks, axis=1), jnp.concatenate(weights, axis=0))
        if p == 0:
            acc_ref[...] = term
        elif p < half - 1:
            acc_ref[...] += term
        else:
            out_ref[...] = (acc_ref[...] + term).astype(BF16)


def project(place, attended, pieces):
    rows = attended.shape[1]
    return pl.pallas_call(
        project_kernel,
        grid=(1,),
        in_specs=[pl.BlockSpec(memory_space=pltpu.SMEM), full(attended.shape, 1)]
        + [pl.BlockSpec(memory_space=pl.ANY)] * len(pieces),
        out_specs=full((rows, D), 1),
        out_shape=jax.ShapeDtypeStruct((rows, D), BF16),
        scratch_shapes=[
            pltpu.VMEM((len(pieces), 256, D), BF16),
            pltpu.VMEM((rows, D), F32),
            pltpu.SemaphoreType.DMA((len(pieces),)),
        ],
        compiler_params=pltpu.CompilerParams(vmem_limit_bytes=20 * MIB),
        cost_estimate=cost(2 * 256 * 2048 * 2048, 10 * MIB),
        name="project",
    )(place, attended, *pieces)


def body(tokens, w_proj, gain, level_codes, w_codes, block_exponent):
    place = lax.axis_index("mp").reshape(1)
    position = lax.axis_index("seq").reshape(1)

    def along_x(block, by):
        return lax.ppermute(block, "mp", [(m, (m // 2 + by) % 4 * 2 + m % 2) for m in range(8)])

    def other_core(block):
        return lax.ppermute(block, "mp", [(m, m ^ 1) for m in range(8)])

    def along_seq(block, to, senders=32):
        return lax.ppermute(block.astype(BF16), "seq", [(i, to(i)) for i in range(senders)])

    after = lax.optimization_barrier
    r = w_proj.reshape(D, 4, 2, 128).transpose(0, 2, 1, 3).reshape(D * 8, 128)

    weight = decode_weight(w_codes, block_exponent)
    gain, weight = after((gain, weight))
    from_left, from_right, from_far = along_x(weight, 1), along_x(weight, -1), along_x(weight, 2)
    weight_other = other_core(weight)
    keys, vt, query, gg, sr, state = projections(r, gain.reshape(1, 256), tokens)

    def inside(part, *earlier):
        return local_levels(part, query, keys, vt, level_codes, sr, *earlier)

    local, sums, reads = (), state.astype(F32), []
    for bit in range(4):
        read = along_seq(sums, lambda i: i ^ (1 << bit))
        local = (inside(bit, *local),)
        read, local = after((read, local))
        sums = sums + read.astype(F32)
        reads.append(read)
    reads.append(along_seq(sums, lambda i: 28 - i // 4 * 4 + i % 4, 16))
    attended = attend(position, query, *local, gg, level_codes, reads)
    attended, from_left, from_right, from_far = after((attended, from_left, from_right, from_far))
    attended = lax.all_to_all(attended.reshape(8, 256, 256), "mp", 0, 0, tiled=True)
    pieces = (weight, from_left, from_right, from_far, weight_other)
    pieces += (other_core(from_left), other_core(from_right), other_core(from_far))
    return project(place, attended, pieces)


def solution(mesh):
    placed = (
        P("seq", None),
        P(None, None, "mp"),
        P("mp"),
        P(None, "mp", "seq"),
        P("mp", None),
        P("mp", None),
    )
    return jax.shard_map(
        body, mesh=mesh, in_specs=placed, out_specs=P(("seq", "mp"), None), check_vma=False
    )
```

```python
import math

import jax
import jax.numpy as jnp
from jax import lax
from jax.experimental import pallas as pl
from jax.experimental.pallas import tpu as pltpu
from jax.sharding import PartitionSpec as P

D = 2048
HEAD_DIM = 128
STRETCH = 64
BLOCK = 128
TILE = 256
F32 = jnp.float32
BF16 = jnp.bfloat16
MIB = 1024 * 1024
VMEM_LIMIT = 60 * MIB


def cost(flops, size):
    return pl.CostEstimate(flops=int(flops), bytes_accessed=int(size), transcendentals=0)


def full(shape, buffers=2):
    zeros = (0,) * len(shape)
    return pl.BlockSpec(shape, lambda *_: zeros, pipeline_mode=pl.Buffered(buffers))


def dot(a, b):
    return jnp.dot(a, b, preferred_element_type=F32)


def dot_nt(a, b):
    return lax.dot_general(a, b, (((1,), (1,)), ((), ())), preferred_element_type=F32)


def decode_kernel(exponent_ref, codes_ref, out_ref):
    step = pl.program_id(0)
    blocks = codes_ref.shape[1] // BLOCK
    for half in range(2):
        rows = slice(half * BLOCK, (half + 1) * BLOCK)
        for block in range(blocks):
            lanes = slice(block * BLOCK, (block + 1) * BLOCK)
            codes = codes_ref[rows, lanes]
            power = exponent_ref[half, step * blocks + block] + 16
            scale = jnp.left_shift(jnp.int32(1), power).astype(F32) * jnp.float32(2.0 ** (-26))
            size = jnp.left_shift(8 + (codes & 7), (codes >> 3) & 15)
            size = jnp.where(codes >= 128, -size, size).astype(F32)
            out_ref[rows, lanes] = (size * scale).astype(BF16)


def decode_weight(codes, exponents):
    columns = 1024
    return pl.pallas_call(
        decode_kernel,
        grid=(D // columns,),
        in_specs=[
            pl.BlockSpec(memory_space=pltpu.SMEM),
            pl.BlockSpec((2 * BLOCK, columns), lambda i: (0, i)),
        ],
        out_specs=pl.BlockSpec((2 * BLOCK, columns), lambda i: (0, i)),
        out_shape=jax.ShapeDtypeStruct((2 * BLOCK, D), BF16),
        compiler_params=pltpu.CompilerParams(vmem_limit_bytes=VMEM_LIMIT),
        cost_estimate=cost(8e6, 3 * MIB),
        name="decode_weight",
    )(exponents, codes)


CHUNKS = 8
ROWS = 512
PARTS = (1, 2, 0, 3)


def unpack_chunk(chunk, parts, r_buf, w_ref, f_ref):
    size = r_buf.shape[0] // CHUNKS
    slot = chunk % f_ref.shape[0]
    f_ref[slot] = r_buf[pl.ds(chunk * size, size), :].astype(F32)
    rows = size // 8
    for at, part in enumerate(parts):
        for half in range(2):
            piece = f_ref[slot, pl.ds(half * 4 + part, rows, stride=8), :]
            w_ref[pl.ds(chunk * rows, rows), pl.ds(at * 256 + half * 128, 128)] = piece.astype(BF16)


def project_tiles(r_hbm, x_hbm, r_buf, x_buf, w_ref, f_ref, acc_ref, r_sem, x_sem, finish):
    size = r_buf.shape[0] // CHUNKS
    deep = w_ref.shape[0] // CHUNKS
    tiles = x_buf.shape[0] // ROWS

    def chunk_copy(chunk):
        at = pl.ds(chunk * size, size)
        return pltpu.make_async_copy(r_hbm.at[at], r_buf.at[at], r_sem.at[chunk])

    def tile_copy(tile):
        at = pl.ds(tile * ROWS, ROWS)
        return pltpu.make_async_copy(x_hbm.at[at], x_buf.at[at], x_sem.at[tile])

    r_copies = [chunk_copy(chunk) for chunk in range(CHUNKS)]
    x_copies = [tile_copy(tile) for tile in range(tiles)]
    for copy in r_copies[:2] + x_copies[:1] + r_copies[2:] + x_copies[1:]:
        copy.start()
    for chunk in range(2):
        r_copies[chunk].wait()
        unpack_chunk(chunk, PARTS, r_buf, w_ref, f_ref)
    x_copies[0].wait()
    for chunk in range(0, CHUNKS, 2):
        later = range(chunk + 2, min(chunk + 4, CHUNKS))
        for ahead in later:
            r_copies[ahead].wait()
        at = pl.ds(chunk * deep, 2 * deep)
        term = dot(x_buf[pl.ds(0, ROWS), at], w_ref[at, :])
        if chunk == 0:
            acc_ref[0] = term
        else:
            acc_ref[0] += term
        for ahead in later:
            unpack_chunk(ahead, PARTS, r_buf, w_ref, f_ref)
    for tile in range(1, tiles):
        x_copies[tile].wait()
        acc_ref[tile % 2] = dot(x_buf[pl.ds(tile * ROWS, ROWS), :], w_ref[...])
        finish(tile - 1)
    finish(tiles - 1)


def projection_scratch(rows):
    return [
        pltpu.VMEM((D * 8, 128), BF16),
        pltpu.VMEM((rows, D), BF16),
        pltpu.VMEM((D, 1024), BF16),
        pltpu.VMEM((2, D * 8 // CHUNKS, 128), F32),
        pltpu.VMEM((2, ROWS, 1024), F32),
        pltpu.SemaphoreType.DMA((CHUNKS,)),
        pltpu.SemaphoreType.DMA((rows // ROWS,)),
    ]


def projections_kernel(r_hbm, gain_ref, x_hbm, k_hbm, vt_hbm, q_hbm, gg_hbm, sr_ref, tot_ref, *scratch):
    *shared, k_buf, vt_buf, q_buf, gg_buf, u_ref, out_sem = scratch
    acc_ref = shared[4]
    copies = []

    def finish(tile):
        rows = pl.ds(tile * ROWS, ROWS)
        keys = acc_ref[tile % 2, :, 0:256].astype(BF16)
        k_buf[rows, :] = keys
        vt = acc_ref[tile % 2, :, 256:512].T.astype(BF16)
        vt_buf[:, rows] = vt
        q_buf[rows, :] = acc_ref[tile % 2, :, 512:768].astype(BF16)
        g = acc_ref[tile % 2, :, 768:1024]
        gg_buf[rows, :] = (gain_ref[...] * (g / (1.0 + jnp.exp(-g)))).astype(BF16)
        for place, (source, target) in enumerate(
            (
                (k_buf.at[rows], k_hbm.at[rows]),
                (vt_buf.at[:, rows], vt_hbm.at[:, rows]),
                (q_buf.at[rows], q_hbm.at[rows]),
                (gg_buf.at[rows], gg_hbm.at[rows]),
            )
        ):
            copy = pltpu.make_async_copy(source, target, out_sem.at[tile, place])
            copy.start()
            copies.append(copy)
        for sub in range(ROWS // TILE):
            at = slice(sub * TILE, (sub + 1) * TILE)
            u = dot(vt[:, at], keys[at])
            for head in range(2):
                lanes = slice(head * 128, (head + 1) * 128)
                u_ref[tile * (ROWS // TILE) + sub, head] = u[lanes, lanes]

    project_tiles(r_hbm, x_hbm, *shared, finish)
    u01 = u_ref[0] + u_ref[1]
    u03 = u01 + (u_ref[2] + u_ref[3])
    u45 = u_ref[4] + u_ref[5]
    for at, tile in enumerate((0, 2, 4, 6)):
        sr_ref[at] = u_ref[tile].astype(BF16)
    sr_ref[4] = u01.astype(BF16)
    sr_ref[5] = u45.astype(BF16)
    sr_ref[6] = u03.astype(BF16)
    tot_ref[...] = (u03 + (u45 + (u_ref[6] + u_ref[7]))).astype(BF16)
    for copy in copies:
        copy.wait()


def projections(r, gain, tokens):
    rows = tokens.shape[0]
    anywhere = pl.BlockSpec(memory_space=pl.ANY)
    return pl.pallas_call(
        projections_kernel,
        grid=(1,),
        in_specs=[anywhere, full((1, 256), 1), anywhere],
        out_specs=[anywhere] * 4 + [full((7, 2, 128, 128), 1), full((2, 128, 128), 1)],
        out_shape=[
            jax.ShapeDtypeStruct((rows, 256), BF16),
            jax.ShapeDtypeStruct((256, rows), BF16),
            jax.ShapeDtypeStruct((rows, 256), BF16),
            jax.ShapeDtypeStruct((rows, 256), BF16),
            jax.ShapeDtypeStruct((7, 2, 128, 128), BF16),
            jax.ShapeDtypeStruct((2, 128, 128), BF16),
        ],
        scratch_shapes=projection_scratch(rows)
        + [
            pltpu.VMEM((rows, 256), BF16),
            pltpu.VMEM((256, rows), BF16),
            pltpu.VMEM((rows, 256), BF16),
            pltpu.VMEM((rows, 256), BF16),
            pltpu.VMEM((8, 2, 128, 128), F32),
            pltpu.SemaphoreType.DMA((rows // ROWS, 4)),
        ],
        compiler_params=pltpu.CompilerParams(vmem_limit_bytes=VMEM_LIMIT),
        cost_estimate=cost(2 * rows * D * 1024, 18 * MIB),
        name="projections",
    )(r, gain, tokens)


def level_scale(span):
    return 1.0 / (128.0 * math.sqrt(HEAD_DIM * span))


def local_kernel(start, q_ref, k_ref, vt_ref, codes_ref, sr_ref, *rest):
    out_ref = rest[-1]
    subs = q_ref.shape[0] // TILE
    s = lax.broadcasted_iota(jnp.int32, (TILE, TILE), 0)
    t = lax.broadcasted_iota(jnp.int32, (TILE, TILE), 1)
    gap = (t >> 6) - (s >> 6)
    inside = (gap == 0) & (s <= t)
    odd = (gap == 1) & ((t >> 6) & 1 == 1)
    second = ((t >> 7) - (s >> 7) == 1)
    for sub in range(subs):
        tile = start + sub
        at = slice(sub * TILE, (sub + 1) * TILE)
        flags = [float((tile >> bit) & 1) for bit in range(3)]
        reads = (tile >> 1, 4 + (tile >> 2), 6)
        for head in range(2):
            lanes = slice(head * 128, (head + 1) * 128)

            def row(level, span, head=head, at=at):
                return codes_ref[level, head : head + 1, at].astype(F32) * level_scale(span)

            left = jnp.concatenate(
                [k_ref[at, lanes]] + [sr_ref[r, head] for r, flag in zip(reads, flags) if flag], axis=0
            )
            product = dot_nt(left, q_ref[at, lanes])
            weight = jnp.where(
                inside,
                row(0, STRETCH),
                jnp.where(
                    odd, row(1, STRETCH), jnp.where(second, row(2, 2 * STRETCH), 0.0)
                ),
            )
            masked = (product[:TILE] * weight).astype(BF16)
            total = dot(vt_ref[lanes, at], masked)
            levels = [j for j in range(3) if flags[j]]
            for place, j in enumerate(levels):
                rows = slice(TILE + place * 128, TILE + (place + 1) * 128)
                total += row(3 + j, TILE << j) * product[rows]
            out_ref[lanes, at] = total.astype(BF16)


def local_levels(part, query, keys, vt, codes, sr, *earlier):
    rows = query.shape[0]
    return pl.pallas_call(
        lambda *refs: local_kernel(part * (ROWS // TILE), *refs),
        grid=(1,),
        in_specs=[
            pl.BlockSpec((ROWS, 256), lambda i: (part, 0), pipeline_mode=pl.Buffered(1)),
            pl.BlockSpec((ROWS, 256), lambda i: (part, 0), pipeline_mode=pl.Buffered(1)),
            pl.BlockSpec((256, ROWS), lambda i: (0, part), pipeline_mode=pl.Buffered(1)),
            pl.BlockSpec((11, 2, ROWS), lambda i: (0, 0, part), pipeline_mode=pl.Buffered(1)),
            full(sr.shape, 1),
        ]
        + [pl.BlockSpec(memory_space=pl.ANY)] * len(earlier),
        out_specs=pl.BlockSpec((256, ROWS), lambda i: (0, part), pipeline_mode=pl.Buffered(1)),
        out_shape=jax.ShapeDtypeStruct((256, rows), BF16),
        input_output_aliases={5: 0} if earlier else {},
        compiler_params=pltpu.CompilerParams(vmem_limit_bytes=VMEM_LIMIT),
        cost_estimate=cost(3e9, 2 * MIB),
        name=f"local_levels_{part}",
    )(query, keys, vt, codes, sr, *earlier)


def attend_kernel(rows_here, at_ref, q_ref, m_ref, gg_ref, codes_ref, *refs):
    *read_refs, out_ref, sd_ref = refs
    position = at_ref[0]

    @pl.when(pl.program_id(0) == 0)
    def _():
        for j, read_ref in enumerate(read_refs):
            for head in range(2):
                sd_ref[head, pl.ds(j * 128, 128), :] = read_ref[head]

    for head in range(2):
        lanes = slice(head * 128, (head + 1) * 128)
        product = dot_nt(sd_ref[head], q_ref[:, lanes])
        memory = m_ref[lanes, :].astype(F32)
        for j in range(5):
            scale = ((position >> j) & 1).astype(F32) * level_scale(rows_here << j)
            row = codes_ref[6 + j, head : head + 1, :].astype(F32) * scale
            memory += row * product[j * 128 : (j + 1) * 128]
        mean = jnp.mean(memory * memory, axis=0, keepdims=True)
        normed = memory * lax.rsqrt(mean + 1e-06)
        out_ref[:, lanes] = (normed.T * gg_ref[:, lanes].astype(F32)).astype(BF16)


def attend(position, query, local, gg, codes, reads):
    rows = query.shape[0]
    tile = 1024
    return pl.pallas_call(
        lambda *refs: attend_kernel(rows, *refs),
        grid=(rows // tile,),
        in_specs=[
            pl.BlockSpec(memory_space=pltpu.SMEM),
            pl.BlockSpec((tile, 256), lambda i: (i, 0)),
            pl.BlockSpec((256, tile), lambda i: (0, i)),
            pl.BlockSpec((tile, 256), lambda i: (i, 0)),
            pl.BlockSpec((11, 2, tile), lambda i: (0, 0, i)),
        ]
        + [full(read.shape, 1) for read in reads],
        out_specs=pl.BlockSpec((tile, 256), lambda i: (i, 0)),
        out_shape=jax.ShapeDtypeStruct((rows, 256), BF16),
        scratch_shapes=[pltpu.VMEM((2, 640, 128), BF16)],
        compiler_params=pltpu.CompilerParams(vmem_limit_bytes=VMEM_LIMIT),
        cost_estimate=cost(3e9, 6 * MIB),
        name="attend",
    )(position, query, local, gg, codes, *reads)


def project_kernel(at_ref, a_ref, *refs):
    pieces, (out_ref, buf, acc_ref, sem) = refs[:-4], refs[-4:]
    x, core = at_ref[0] >> 1, at_ref[0] & 1
    copies = [pltpu.make_async_copy(piece, buf.at[p], sem.at[p]) for p, piece in enumerate(pieces)]
    for copy in copies:
        copy.start()
    half = len(pieces) // 2
    for p in range(half):
        blocks, weights = [], []
        for flip in range(2):
            copies[p + flip * half].wait()
            blocks.append(a_ref[((x + (0, 3, 1, 2)[p]) & 3) * 2 + (core ^ flip)])
            weights.append(buf[p + flip * half])
        term = dot(jnp.concatenate(blocks, axis=1), jnp.concatenate(weights, axis=0))
        if p == 0:
            acc_ref[...] = term
        elif p < half - 1:
            acc_ref[...] += term
        else:
            out_ref[...] = (acc_ref[...] + term).astype(BF16)


def project(place, attended, pieces):
    rows = attended.shape[1]
    return pl.pallas_call(
        project_kernel,
        grid=(1,),
        in_specs=[pl.BlockSpec(memory_space=pltpu.SMEM), full(attended.shape, 1)]
        + [pl.BlockSpec(memory_space=pl.ANY)] * len(pieces),
        out_specs=full((rows, D), 1),
        out_shape=jax.ShapeDtypeStruct((rows, D), BF16),
        scratch_shapes=[
            pltpu.VMEM((len(pieces), 256, D), BF16),
            pltpu.VMEM((rows, D), F32),
            pltpu.SemaphoreType.DMA((len(pieces),)),
        ],
        compiler_params=pltpu.CompilerParams(vmem_limit_bytes=20 * MIB),
        cost_estimate=cost(2 * 256 * 2048 * 2048, 10 * MIB),
        name="project",
    )(place, attended, *pieces)


def body(tokens, w_proj, gain, level_codes, w_codes, block_exponent):
    place = lax.axis_index("mp").reshape(1)
    position = lax.axis_index("seq").reshape(1)

    def along_x(block, by):
        return lax.ppermute(block, "mp", [(m, (m // 2 + by) % 4 * 2 + m % 2) for m in range(8)])

    def other_core(block):
        return lax.ppermute(block, "mp", [(m, m ^ 1) for m in range(8)])

    def along_seq(block, to, senders=32):
        return lax.ppermute(block.astype(BF16), "seq", [(i, to(i)) for i in range(senders)])

    after = lax.optimization_barrier
    r = w_proj.reshape(D, 4, 2, 128).transpose(0, 2, 1, 3).reshape(D * 8, 128)

    weight = decode_weight(w_codes, block_exponent)
    gain, weight = after((gain, weight))
    from_left, from_right, from_far = along_x(weight, 1), along_x(weight, -1), along_x(weight, 2)
    keys, vt, query, gg, sr, state = projections(r, gain.reshape(1, 256), tokens)

    def inside(part, *earlier):
        return local_levels(part, query, keys, vt, level_codes, sr, *earlier)

    local, sums, reads = (), state.astype(F32), []
    for bit in range(4):
        read = along_seq(sums, lambda i: i ^ (1 << bit))
        local = (inside(bit, *local),)
        read, local = after((read, local))
        sums = sums + read.astype(F32)
        reads.append(read)
    reads.append(along_seq(sums, lambda i: 28 - i // 4 * 4 + i % 4, 16))
    attended = attend(position, query, *local, gg, level_codes, reads)
    attended, *pieces = after((attended, weight, from_left, from_right, from_far))
    attended = lax.all_to_all(attended.reshape(8, 256, 256), "mp", 0, 0, tiled=True)
    return project(place, attended, pieces + [other_core(piece) for piece in pieces])


def solution(mesh):
    placed = (
        P("seq", None),
        P(None, None, "mp"),
        P("mp"),
        P(None, "mp", "seq"),
        P("mp", None),
        P("mp", None),
    )
    return jax.shard_map(
        body, mesh=mesh, in_specs=placed, out_specs=P(("seq", "mp"), None), check_vma=False
    )
```

```python
import math

import jax
import jax.numpy as jnp
from jax import lax
from jax.experimental import pallas as pl
from jax.experimental.pallas import tpu as pltpu
from jax.sharding import PartitionSpec as P

D = 2048
HEAD_DIM = 128
STRETCH = 64
BLOCK = 128
TILE = 256
F32 = jnp.float32
BF16 = jnp.bfloat16
MIB = 1024 * 1024
VMEM_LIMIT = 60 * MIB


def cost(flops, size):
    return pl.CostEstimate(flops=int(flops), bytes_accessed=int(size), transcendentals=0)


def full(shape, buffers=2):
    zeros = (0,) * len(shape)
    return pl.BlockSpec(shape, lambda *_: zeros, pipeline_mode=pl.Buffered(buffers))


def dot(a, b):
    return jnp.dot(a, b, preferred_element_type=F32)


def dot_nt(a, b):
    return lax.dot_general(a, b, (((1,), (1,)), ((), ())), preferred_element_type=F32)


def decode_kernel(exponent_ref, codes_ref, out_ref):
    step = pl.program_id(0)
    blocks = codes_ref.shape[1] // BLOCK
    for half in range(2):
        rows = slice(half * BLOCK, (half + 1) * BLOCK)
        for block in range(blocks):
            lanes = slice(block * BLOCK, (block + 1) * BLOCK)
            codes = codes_ref[rows, lanes]
            power = exponent_ref[half, step * blocks + block] + 16
            scale = jnp.left_shift(jnp.int32(1), power).astype(F32) * jnp.float32(2.0 ** (-26))
            size = jnp.left_shift(8 + (codes & 7), (codes >> 3) & 15)
            size = jnp.where(codes >= 128, -size, size).astype(F32)
            out_ref[rows, lanes] = (size * scale).astype(BF16)


def decode_weight(codes, exponents):
    columns = 1024
    return pl.pallas_call(
        decode_kernel,
        grid=(D // columns,),
        in_specs=[
            pl.BlockSpec(memory_space=pltpu.SMEM),
            pl.BlockSpec((2 * BLOCK, columns), lambda i: (0, i)),
        ],
        out_specs=pl.BlockSpec((2 * BLOCK, columns), lambda i: (0, i)),
        out_shape=jax.ShapeDtypeStruct((2 * BLOCK, D), BF16),
        compiler_params=pltpu.CompilerParams(vmem_limit_bytes=VMEM_LIMIT),
        cost_estimate=cost(8e6, 3 * MIB),
        name="decode_weight",
    )(exponents, codes)


CHUNKS = 8
ROWS = 512
PARTS = (1, 2, 0, 3)


def unpack_chunk(chunk, parts, r_buf, w_ref, f_ref):
    size = r_buf.shape[0] // CHUNKS
    slot = chunk % f_ref.shape[0]
    f_ref[slot] = r_buf[pl.ds(chunk * size, size), :].astype(F32)
    rows = size // 8
    for at, part in enumerate(parts):
        for half in range(2):
            piece = f_ref[slot, pl.ds(half * 4 + part, rows, stride=8), :]
            w_ref[pl.ds(chunk * rows, rows), pl.ds(at * 256 + half * 128, 128)] = piece.astype(BF16)


def project_tiles(r_hbm, x_hbm, r_buf, x_buf, w_ref, f_ref, acc_ref, r_sem, x_sem, finish):
    size = r_buf.shape[0] // CHUNKS
    deep = w_ref.shape[0] // CHUNKS
    tiles = x_buf.shape[0] // ROWS

    def chunk_copy(chunk):
        at = pl.ds(chunk * size, size)
        return pltpu.make_async_copy(r_hbm.at[at], r_buf.at[at], r_sem.at[chunk])

    def tile_copy(tile):
        at = pl.ds(tile * ROWS, ROWS)
        return pltpu.make_async_copy(x_hbm.at[at], x_buf.at[at], x_sem.at[tile])

    r_copies = [chunk_copy(chunk) for chunk in range(CHUNKS)]
    x_copies = [tile_copy(tile) for tile in range(tiles)]
    for copy in r_copies[:2] + x_copies[:1] + r_copies[2:] + x_copies[1:]:
        copy.start()
    for chunk in range(2):
        r_copies[chunk].wait()
        unpack_chunk(chunk, PARTS, r_buf, w_ref, f_ref)
    x_copies[0].wait()
    for chunk in range(0, CHUNKS, 2):
        later = range(chunk + 2, min(chunk + 4, CHUNKS))
        for ahead in later:
            r_copies[ahead].wait()
        at = pl.ds(chunk * deep, 2 * deep)
        term = dot(x_buf[pl.ds(0, ROWS), at], w_ref[at, :])
        if chunk == 0:
            acc_ref[0] = term
        else:
            acc_ref[0] += term
        for ahead in later:
            unpack_chunk(ahead, PARTS, r_buf, w_ref, f_ref)
    for tile in range(1, tiles):
        x_copies[tile].wait()
        acc_ref[tile % 2] = dot(x_buf[pl.ds(tile * ROWS, ROWS), :], w_ref[...])
        finish(tile - 1)
    finish(tiles - 1)


def projection_scratch(rows):
    return [
        pltpu.VMEM((D * 8, 128), BF16),
        pltpu.VMEM((rows, D), BF16),
        pltpu.VMEM((D, 1024), BF16),
        pltpu.VMEM((2, D * 8 // CHUNKS, 128), F32),
        pltpu.VMEM((2, ROWS, 1024), F32),
        pltpu.SemaphoreType.DMA((CHUNKS,)),
        pltpu.SemaphoreType.DMA((rows // ROWS,)),
    ]


def projections_kernel(r_hbm, gain_ref, x_hbm, k_hbm, vt_hbm, q_hbm, gg_hbm, sr_ref, tot_ref, *scratch):
    *shared, k_buf, vt_buf, q_buf, gg_buf, u_ref, out_sem = scratch
    acc_ref = shared[4]
    copies = []

    def finish(tile):
        rows = pl.ds(tile * ROWS, ROWS)
        keys = acc_ref[tile % 2, :, 0:256].astype(BF16)
        k_buf[rows, :] = keys
        vt = acc_ref[tile % 2, :, 256:512].T.astype(BF16)
        vt_buf[:, rows] = vt
        q_buf[rows, :] = acc_ref[tile % 2, :, 512:768].astype(BF16)
        g = acc_ref[tile % 2, :, 768:1024]
        gg_buf[rows, :] = (gain_ref[...] * (g / (1.0 + jnp.exp(-g)))).astype(BF16)
        for place, (source, target) in enumerate(
            (
                (k_buf.at[rows], k_hbm.at[rows]),
                (vt_buf.at[:, rows], vt_hbm.at[:, rows]),
                (q_buf.at[rows], q_hbm.at[rows]),
                (gg_buf.at[rows], gg_hbm.at[rows]),
            )
        ):
            copy = pltpu.make_async_copy(source, target, out_sem.at[tile, place])
            copy.start()
            copies.append(copy)
        for sub in range(ROWS // TILE):
            at = slice(sub * TILE, (sub + 1) * TILE)
            u = dot(vt[:, at], keys[at])
            for head in range(2):
                lanes = slice(head * 128, (head + 1) * 128)
                u_ref[tile * (ROWS // TILE) + sub, head] = u[lanes, lanes]

    project_tiles(r_hbm, x_hbm, *shared, finish)
    u01 = u_ref[0] + u_ref[1]
    u03 = u01 + (u_ref[2] + u_ref[3])
    u45 = u_ref[4] + u_ref[5]
    for at, tile in enumerate((0, 2, 4, 6)):
        sr_ref[at] = u_ref[tile].astype(BF16)
    sr_ref[4] = u01.astype(BF16)
    sr_ref[5] = u45.astype(BF16)
    sr_ref[6] = u03.astype(BF16)
    tot_ref[...] = (u03 + (u45 + (u_ref[6] + u_ref[7]))).astype(BF16)
    for copy in copies:
        copy.wait()


def projections(r, gain, tokens):
    rows = tokens.shape[0]
    anywhere = pl.BlockSpec(memory_space=pl.ANY)
    return pl.pallas_call(
        projections_kernel,
        grid=(1,),
        in_specs=[anywhere, full((1, 256), 1), anywhere],
        out_specs=[anywhere] * 4 + [full((7, 2, 128, 128), 1), full((2, 128, 128), 1)],
        out_shape=[
            jax.ShapeDtypeStruct((rows, 256), BF16),
            jax.ShapeDtypeStruct((256, rows), BF16),
            jax.ShapeDtypeStruct((rows, 256), BF16),
            jax.ShapeDtypeStruct((rows, 256), BF16),
            jax.ShapeDtypeStruct((7, 2, 128, 128), BF16),
            jax.ShapeDtypeStruct((2, 128, 128), BF16),
        ],
        scratch_shapes=projection_scratch(rows)
        + [
            pltpu.VMEM((rows, 256), BF16),
            pltpu.VMEM((256, rows), BF16),
            pltpu.VMEM((rows, 256), BF16),
            pltpu.VMEM((rows, 256), BF16),
            pltpu.VMEM((8, 2, 128, 128), F32),
            pltpu.SemaphoreType.DMA((rows // ROWS, 4)),
        ],
        compiler_params=pltpu.CompilerParams(vmem_limit_bytes=VMEM_LIMIT),
        cost_estimate=cost(2 * rows * D * 1024, 18 * MIB),
        name="projections",
    )(r, gain, tokens)


def level_scale(span):
    return 1.0 / (128.0 * math.sqrt(HEAD_DIM * span))


def local_kernel(start, q_ref, k_ref, vt_ref, codes_ref, sr_ref, *rest):
    out_ref = rest[-1]
    subs = q_ref.shape[0] // TILE
    s = lax.broadcasted_iota(jnp.int32, (TILE, TILE), 0)
    t = lax.broadcasted_iota(jnp.int32, (TILE, TILE), 1)
    gap = (t >> 6) - (s >> 6)
    inside = (gap == 0) & (s <= t)
    odd = (gap == 1) & ((t >> 6) & 1 == 1)
    second = ((t >> 7) - (s >> 7) == 1)
    for sub in range(subs):
        tile = start + sub
        at = slice(sub * TILE, (sub + 1) * TILE)
        flags = [float((tile >> bit) & 1) for bit in range(3)]
        reads = (tile >> 1, 4 + (tile >> 2), 6)
        for head in range(2):
            lanes = slice(head * 128, (head + 1) * 128)

            def row(level, span, head=head, at=at):
                return codes_ref[level, head : head + 1, at].astype(F32) * level_scale(span)

            left = jnp.concatenate(
                [k_ref[at, lanes]] + [sr_ref[r, head] for r, flag in zip(reads, flags) if flag], axis=0
            )
            product = dot_nt(left, q_ref[at, lanes])
            weight = jnp.where(
                inside,
                row(0, STRETCH),
                jnp.where(
                    odd, row(1, STRETCH), jnp.where(second, row(2, 2 * STRETCH), 0.0)
                ),
            )
            masked = (product[:TILE] * weight).astype(BF16)
            total = dot(vt_ref[lanes, at], masked)
            levels = [j for j in range(3) if flags[j]]
            for place, j in enumerate(levels):
                rows = slice(TILE + place * 128, TILE + (place + 1) * 128)
                total += row(3 + j, TILE << j) * product[rows]
            out_ref[lanes, at] = total.astype(BF16)


def local_levels(part, query, keys, vt, codes, sr, *earlier):
    rows = query.shape[0]
    return pl.pallas_call(
        lambda *refs: local_kernel(part * (ROWS // TILE), *refs),
        grid=(1,),
        in_specs=[
            pl.BlockSpec((ROWS, 256), lambda i: (part, 0), pipeline_mode=pl.Buffered(1)),
            pl.BlockSpec((ROWS, 256), lambda i: (part, 0), pipeline_mode=pl.Buffered(1)),
            pl.BlockSpec((256, ROWS), lambda i: (0, part), pipeline_mode=pl.Buffered(1)),
            pl.BlockSpec((11, 2, ROWS), lambda i: (0, 0, part), pipeline_mode=pl.Buffered(1)),
            full(sr.shape, 1),
        ]
        + [pl.BlockSpec(memory_space=pl.ANY)] * len(earlier),
        out_specs=pl.BlockSpec((256, ROWS), lambda i: (0, part), pipeline_mode=pl.Buffered(1)),
        out_shape=jax.ShapeDtypeStruct((256, rows), BF16),
        input_output_aliases={5: 0} if earlier else {},
        compiler_params=pltpu.CompilerParams(vmem_limit_bytes=VMEM_LIMIT),
        cost_estimate=cost(3e9, 2 * MIB),
        name=f"local_levels_{part}",
    )(query, keys, vt, codes, sr, *earlier)


def attend_kernel(rows_here, at_ref, q_ref, m_ref, gg_ref, codes_ref, *refs):
    *read_refs, out_ref, sd_ref = refs
    position = at_ref[0]

    @pl.when(pl.program_id(0) == 0)
    def _():
        for j, read_ref in enumerate(read_refs):
            for head in range(2):
                sd_ref[head, pl.ds(j * 128, 128), :] = read_ref[head]

    for head in range(2):
        lanes = slice(head * 128, (head + 1) * 128)
        product = dot_nt(sd_ref[head], q_ref[:, lanes])
        memory = m_ref[lanes, :].astype(F32)
        for j in range(5):
            scale = ((position >> j) & 1).astype(F32) * level_scale(rows_here << j)
            row = codes_ref[6 + j, head : head + 1, :].astype(F32) * scale
            memory += row * product[j * 128 : (j + 1) * 128]
        mean = jnp.mean(memory * memory, axis=0, keepdims=True)
        normed = memory * lax.rsqrt(mean + 1e-06)
        out_ref[:, lanes] = (normed.T * gg_ref[:, lanes].astype(F32)).astype(BF16)


def attend(position, query, local, gg, codes, reads):
    rows = query.shape[0]
    tile = 1024
    return pl.pallas_call(
        lambda *refs: attend_kernel(rows, *refs),
        grid=(rows // tile,),
        in_specs=[
            pl.BlockSpec(memory_space=pltpu.SMEM),
            pl.BlockSpec((tile, 256), lambda i: (i, 0)),
            pl.BlockSpec((256, tile), lambda i: (0, i)),
            pl.BlockSpec((tile, 256), lambda i: (i, 0)),
            pl.BlockSpec((11, 2, tile), lambda i: (0, 0, i)),
        ]
        + [full(read.shape, 1) for read in reads],
        out_specs=pl.BlockSpec((tile, 256), lambda i: (i, 0)),
        out_shape=jax.ShapeDtypeStruct((rows, 256), BF16),
        scratch_shapes=[pltpu.VMEM((2, 640, 128), BF16)],
        compiler_params=pltpu.CompilerParams(vmem_limit_bytes=VMEM_LIMIT),
        cost_estimate=cost(3e9, 6 * MIB),
        name="attend",
    )(position, query, local, gg, codes, *reads)


def project_kernel(at_ref, a_ref, *refs):
    pieces, (out_ref, buf, acc_ref, sem) = refs[:-4], refs[-4:]
    x, core = at_ref[0] >> 1, at_ref[0] & 1
    copies = [pltpu.make_async_copy(piece, buf.at[p], sem.at[p]) for p, piece in enumerate(pieces)]
    half = len(pieces) // 2
    for p in range(half):
        copies[p].start()
        copies[p + half].start()
    for p in range(half):
        blocks, weights = [], []
        for flip in range(2):
            copies[p + flip * half].wait()
            blocks.append(a_ref[((x + (0, 3, 1, 2)[p]) & 3) * 2 + (core ^ flip)])
            weights.append(buf[p + flip * half])
        term = dot(jnp.concatenate(blocks, axis=1), jnp.concatenate(weights, axis=0))
        if p == 0:
            acc_ref[...] = term
        elif p < half - 1:
            acc_ref[...] += term
        else:
            out_ref[...] = (acc_ref[...] + term).astype(BF16)


def project(place, attended, pieces):
    rows = attended.shape[1]
    return pl.pallas_call(
        project_kernel,
        grid=(1,),
        in_specs=[pl.BlockSpec(memory_space=pltpu.SMEM), full(attended.shape, 1)]
        + [pl.BlockSpec(memory_space=pl.ANY)] * len(pieces),
        out_specs=full((rows, D), 1),
        out_shape=jax.ShapeDtypeStruct((rows, D), BF16),
        scratch_shapes=[
            pltpu.VMEM((len(pieces), 256, D), BF16),
            pltpu.VMEM((rows, D), F32),
            pltpu.SemaphoreType.DMA((len(pieces),)),
        ],
        compiler_params=pltpu.CompilerParams(vmem_limit_bytes=20 * MIB),
        cost_estimate=cost(2 * 256 * 2048 * 2048, 10 * MIB),
        name="project",
    )(place, attended, *pieces)


def body(tokens, w_proj, gain, level_codes, w_codes, block_exponent):
    place = lax.axis_index("mp").reshape(1)
    position = lax.axis_index("seq").reshape(1)

    def along_x(block, by):
        return lax.ppermute(block, "mp", [(m, (m // 2 + by) % 4 * 2 + m % 2) for m in range(8)])

    def other_core(block):
        return lax.ppermute(block, "mp", [(m, m ^ 1) for m in range(8)])

    def along_seq(block, to, senders=32):
        return lax.ppermute(block.astype(BF16), "seq", [(i, to(i)) for i in range(senders)])

    after = lax.optimization_barrier
    r = w_proj.reshape(D, 4, 2, 128).transpose(0, 2, 1, 3).reshape(D * 8, 128)

    weight = decode_weight(w_codes, block_exponent)
    gain, weight = after((gain, weight))
    from_left, from_right, from_far = along_x(weight, 1), along_x(weight, -1), along_x(weight, 2)
    keys, vt, query, gg, sr, state = projections(r, gain.reshape(1, 256), tokens)

    def inside(part, *earlier):
        return local_levels(part, query, keys, vt, level_codes, sr, *earlier)

    local, sums, reads = (), state.astype(F32), []
    for bit in range(4):
        read = along_seq(sums, lambda i: i ^ (1 << bit))
        local = (inside(bit, *local),)
        read, local = after((read, local))
        sums = sums + read.astype(F32)
        reads.append(read)
    reads.append(along_seq(sums, lambda i: 28 - i // 4 * 4 + i % 4, 16))
    attended = attend(position, query, *local, gg, level_codes, reads)
    attended, *pieces = after((attended, weight, from_left, from_right, from_far))
    attended = lax.all_to_all(attended.reshape(8, 256, 256), "mp", 0, 0, tiled=True)
    return project(place, attended, pieces + [other_core(piece) for piece in pieces])


def solution(mesh):
    placed = (
        P("seq", None),
        P(None, None, "mp"),
        P("mp"),
        P(None, "mp", "seq"),
        P("mp", None),
        P("mp", None),
    )
    return jax.shard_map(
        body, mesh=mesh, in_specs=placed, out_specs=P(("seq", "mp"), None), check_vma=False
    )
```

```python
import math

import jax
import jax.numpy as jnp
from jax import lax
from jax.experimental import pallas as pl
from jax.experimental.pallas import tpu as pltpu
from jax.sharding import PartitionSpec as P

D = 2048
HEAD_DIM = 128
STRETCH = 64
BLOCK = 128
TILE = 256
F32 = jnp.float32
BF16 = jnp.bfloat16
MIB = 1024 * 1024
VMEM_LIMIT = 60 * MIB


def cost(flops, size):
    return pl.CostEstimate(flops=int(flops), bytes_accessed=int(size), transcendentals=0)


def full(shape, buffers=2):
    zeros = (0,) * len(shape)
    return pl.BlockSpec(shape, lambda *_: zeros, pipeline_mode=pl.Buffered(buffers))


def dot(a, b):
    return jnp.dot(a, b, preferred_element_type=F32)


def dot_nt(a, b):
    return lax.dot_general(a, b, (((1,), (1,)), ((), ())), preferred_element_type=F32)


def decode_kernel(exponent_ref, codes_ref, out_ref):
    for block in range(codes_ref.shape[1] // BLOCK):
        lanes = slice(block * BLOCK, (block + 1) * BLOCK)
        codes = codes_ref[:, lanes]
        power = exponent_ref[pl.program_id(0), block] + 16
        scale = jnp.left_shift(jnp.int32(1), power).astype(F32) * jnp.float32(2.0 ** (-26))
        size = jnp.left_shift(8 + (codes & 7), (codes >> 3) & 15)
        size = jnp.where(codes >= 128, -size, size).astype(F32)
        out_ref[:, lanes] = (size * scale).astype(BF16)


def decode_weight(codes, exponents):
    rows = pl.BlockSpec((BLOCK, D), lambda i: (i, 0))
    return pl.pallas_call(
        decode_kernel,
        grid=(codes.shape[0] // BLOCK,),
        in_specs=[pl.BlockSpec(memory_space=pltpu.SMEM), rows],
        out_specs=rows,
        out_shape=jax.ShapeDtypeStruct(codes.shape, BF16),
        compiler_params=pltpu.CompilerParams(vmem_limit_bytes=VMEM_LIMIT),
        cost_estimate=cost(8e6, 3 * MIB),
        name="decode_weight",
    )(exponents, codes)


CHUNKS = 8
ROWS = 512
PARTS = (1, 2, 0, 3)


def unpack_chunk(chunk, parts, r_buf, w_ref, f_ref):
    size = r_buf.shape[0] // CHUNKS
    slot = chunk % f_ref.shape[0]
    f_ref[slot] = r_buf[pl.ds(chunk * size, size), :].astype(F32)
    rows = size // 8
    for at, part in enumerate(parts):
        for half in range(2):
            piece = f_ref[slot, pl.ds(half * 4 + part, rows, stride=8), :]
            w_ref[pl.ds(chunk * rows, rows), pl.ds(at * 256 + half * 128, 128)] = piece.astype(BF16)


def project_tiles(r_hbm, x_hbm, r_buf, x_buf, w_ref, f_ref, acc_ref, r_sem, x_sem, finish):
    size = r_buf.shape[0] // CHUNKS
    deep = w_ref.shape[0] // CHUNKS
    tiles = x_buf.shape[0] // ROWS

    def chunk_copy(chunk):
        at = pl.ds(chunk * size, size)
        return pltpu.make_async_copy(r_hbm.at[at], r_buf.at[at], r_sem.at[chunk])

    def tile_copy(tile):
        at = pl.ds(tile * ROWS, ROWS)
        return pltpu.make_async_copy(x_hbm.at[at], x_buf.at[at], x_sem.at[tile])

    r_copies = [chunk_copy(chunk) for chunk in range(CHUNKS)]
    x_copies = [tile_copy(tile) for tile in range(tiles)]
    for copy in r_copies[:2] + x_copies[:1] + r_copies[2:] + x_copies[1:]:
        copy.start()
    for chunk in range(2):
        r_copies[chunk].wait()
        unpack_chunk(chunk, PARTS, r_buf, w_ref, f_ref)
    x_copies[0].wait()
    for chunk in range(0, CHUNKS, 2):
        later = range(chunk + 2, min(chunk + 4, CHUNKS))
        for ahead in later:
            r_copies[ahead].wait()
        at = pl.ds(chunk * deep, 2 * deep)
        term = dot(x_buf[pl.ds(0, ROWS), at], w_ref[at, :])
        if chunk == 0:
            acc_ref[0] = term
        else:
            acc_ref[0] += term
        for ahead in later:
            unpack_chunk(ahead, PARTS, r_buf, w_ref, f_ref)
    for tile in range(1, tiles):
        x_copies[tile].wait()
        acc_ref[tile % 2] = dot(x_buf[pl.ds(tile * ROWS, ROWS), :], w_ref[...])
        finish(tile - 1)
    finish(tiles - 1)


def projection_scratch(rows):
    return [
        pltpu.VMEM((D * 8, 128), BF16),
        pltpu.VMEM((rows, D), BF16),
        pltpu.VMEM((D, 1024), BF16),
        pltpu.VMEM((2, D * 8 // CHUNKS, 128), F32),
        pltpu.VMEM((2, ROWS, 1024), F32),
        pltpu.SemaphoreType.DMA((CHUNKS,)),
        pltpu.SemaphoreType.DMA((rows // ROWS,)),
    ]


def projections_kernel(r_hbm, gain_ref, x_hbm, k_hbm, vt_hbm, q_hbm, gg_hbm, sr_ref, tot_ref, *scratch):
    *shared, k_buf, vt_buf, q_buf, gg_buf, u_ref, out_sem = scratch
    acc_ref = shared[4]
    copies = []

    def finish(tile):
        rows = pl.ds(tile * ROWS, ROWS)
        keys = acc_ref[tile % 2, :, 0:256].astype(BF16)
        k_buf[rows, :] = keys
        vt = acc_ref[tile % 2, :, 256:512].T.astype(BF16)
        vt_buf[:, rows] = vt
        q_buf[rows, :] = acc_ref[tile % 2, :, 512:768].astype(BF16)
        g = acc_ref[tile % 2, :, 768:1024]
        gg_buf[rows, :] = (gain_ref[...] * (g / (1.0 + jnp.exp(-g)))).astype(BF16)
        for place, (source, target) in enumerate(
            (
                (k_buf.at[rows], k_hbm.at[rows]),
                (vt_buf.at[:, rows], vt_hbm.at[:, rows]),
                (q_buf.at[rows], q_hbm.at[rows]),
                (gg_buf.at[rows], gg_hbm.at[rows]),
            )
        ):
            copy = pltpu.make_async_copy(source, target, out_sem.at[tile, place])
            copy.start()
            copies.append(copy)
        for sub in range(ROWS // TILE):
            at = slice(sub * TILE, (sub + 1) * TILE)
            u = dot(vt[:, at], keys[at])
            for head in range(2):
                lanes = slice(head * 128, (head + 1) * 128)
                u_ref[tile * (ROWS // TILE) + sub, head] = u[lanes, lanes]

    project_tiles(r_hbm, x_hbm, *shared, finish)
    u01 = u_ref[0] + u_ref[1]
    u03 = u01 + (u_ref[2] + u_ref[3])
    u45 = u_ref[4] + u_ref[5]
    for at, tile in enumerate((0, 2, 4, 6)):
        sr_ref[at] = u_ref[tile].astype(BF16)
    sr_ref[4] = u01.astype(BF16)
    sr_ref[5] = u45.astype(BF16)
    sr_ref[6] = u03.astype(BF16)
    tot_ref[...] = (u03 + (u45 + (u_ref[6] + u_ref[7]))).astype(BF16)
    for copy in copies:
        copy.wait()


def projections(r, gain, tokens):
    rows = tokens.shape[0]
    anywhere = pl.BlockSpec(memory_space=pl.ANY)
    return pl.pallas_call(
        projections_kernel,
        grid=(1,),
        in_specs=[anywhere, full((1, 256), 1), anywhere],
        out_specs=[anywhere] * 4 + [full((7, 2, 128, 128), 1), full((2, 128, 128), 1)],
        out_shape=[
            jax.ShapeDtypeStruct((rows, 256), BF16),
            jax.ShapeDtypeStruct((256, rows), BF16),
            jax.ShapeDtypeStruct((rows, 256), BF16),
            jax.ShapeDtypeStruct((rows, 256), BF16),
            jax.ShapeDtypeStruct((7, 2, 128, 128), BF16),
            jax.ShapeDtypeStruct((2, 128, 128), BF16),
        ],
        scratch_shapes=projection_scratch(rows)
        + [
            pltpu.VMEM((rows, 256), BF16),
            pltpu.VMEM((256, rows), BF16),
            pltpu.VMEM((rows, 256), BF16),
            pltpu.VMEM((rows, 256), BF16),
            pltpu.VMEM((8, 2, 128, 128), F32),
            pltpu.SemaphoreType.DMA((rows // ROWS, 4)),
        ],
        compiler_params=pltpu.CompilerParams(vmem_limit_bytes=VMEM_LIMIT),
        cost_estimate=cost(2 * rows * D * 1024, 18 * MIB),
        name="projections",
    )(r, gain, tokens)


def level_scale(span):
    return 1.0 / (128.0 * math.sqrt(HEAD_DIM * span))


def local_kernel(start, picks, q_ref, k_ref, vt_ref, codes_ref, *rest):
    states, out_ref = dict(zip(picks, rest)), rest[-1]
    subs = q_ref.shape[0] // TILE
    s = lax.broadcasted_iota(jnp.int32, (TILE, TILE), 0)
    t = lax.broadcasted_iota(jnp.int32, (TILE, TILE), 1)
    gap = (t >> 6) - (s >> 6)
    inside = (gap == 0) & (s <= t)
    odd = (gap == 1) & ((t >> 6) & 1 == 1)
    second = ((t >> 7) - (s >> 7) == 1)
    for sub in range(subs):
        tile = start + sub
        at = slice(sub * TILE, (sub + 1) * TILE)
        flags = [float((tile >> bit) & 1) for bit in range(3)]
        reads = (tile >> 1, 4 + (tile >> 2), 6)
        for head in range(2):
            lanes = slice(head * 128, (head + 1) * 128)

            def row(level, span, head=head, at=at):
                return codes_ref[level, head : head + 1, at].astype(F32) * level_scale(span)

            left = jnp.concatenate(
                [k_ref[at, lanes]] + [states[r][0, head] for r, flag in zip(reads, flags) if flag], axis=0
            )
            product = dot_nt(left, q_ref[at, lanes])
            weight = jnp.where(
                inside,
                row(0, STRETCH),
                jnp.where(
                    odd, row(1, STRETCH), jnp.where(second, row(2, 2 * STRETCH), 0.0)
                ),
            )
            masked = (product[:TILE] * weight).astype(BF16)
            total = dot(vt_ref[lanes, at], masked)
            levels = [j for j in range(3) if flags[j]]
            for place, j in enumerate(levels):
                rows = slice(TILE + place * 128, TILE + (place + 1) * 128)
                total += row(3 + j, TILE << j) * product[rows]
            out_ref[lanes, at] = total.astype(BF16)


def local_levels(part, query, keys, vt, codes, sr, *earlier):
    rows = query.shape[0]
    picks = [part] + [4 + part // 2] * (part % 2) + [6] * (part // 2)
    return pl.pallas_call(
        lambda *refs: local_kernel(part * (ROWS // TILE), picks, *refs),
        grid=(1,),
        in_specs=[
            pl.BlockSpec((ROWS, 256), lambda i: (part, 0), pipeline_mode=pl.Buffered(1)),
            pl.BlockSpec((ROWS, 256), lambda i: (part, 0), pipeline_mode=pl.Buffered(1)),
            pl.BlockSpec((256, ROWS), lambda i: (0, part), pipeline_mode=pl.Buffered(1)),
            pl.BlockSpec((11, 2, ROWS), lambda i: (0, 0, part), pipeline_mode=pl.Buffered(1)),
        ]
        + [
            pl.BlockSpec((1, 2, 128, 128), lambda i, pick=pick: (pick, 0, 0, 0), pipeline_mode=pl.Buffered(1))
            for pick in picks
        ]
        + [pl.BlockSpec(memory_space=pl.ANY)] * len(earlier),
        out_specs=pl.BlockSpec((256, ROWS), lambda i: (0, part), pipeline_mode=pl.Buffered(1)),
        out_shape=jax.ShapeDtypeStruct((256, rows), BF16),
        input_output_aliases={4 + len(picks): 0} if earlier else {},
        compiler_params=pltpu.CompilerParams(vmem_limit_bytes=VMEM_LIMIT),
        cost_estimate=cost(3e9, 2 * MIB),
        name=f"local_levels_{part}",
    )(query, keys, vt, codes, *[sr] * len(picks), *earlier)


def attend_kernel(rows_here, at_ref, q_ref, m_ref, gg_ref, codes_ref, *refs):
    *read_refs, out_ref, sd_ref = refs
    position = at_ref[0]

    @pl.when(pl.program_id(0) == 0)
    def _():
        for j, read_ref in enumerate(read_refs):
            for head in range(2):
                sd_ref[head, pl.ds(j * 128, 128), :] = read_ref[head]

    for head in range(2):
        lanes = slice(head * 128, (head + 1) * 128)
        product = dot_nt(sd_ref[head], q_ref[:, lanes])
        memory = m_ref[lanes, :].astype(F32)
        for j in range(5):
            scale = ((position >> j) & 1).astype(F32) * level_scale(rows_here << j)
            row = codes_ref[6 + j, head : head + 1, :].astype(F32) * scale
            memory += row * product[j * 128 : (j + 1) * 128]
        mean = jnp.mean(memory * memory, axis=0, keepdims=True)
        normed = memory * lax.rsqrt(mean + 1e-06)
        out_ref[:, lanes] = (normed.T * gg_ref[:, lanes].astype(F32)).astype(BF16)


def attend(position, query, local, gg, codes, reads):
    rows = query.shape[0]
    tile = 1024
    return pl.pallas_call(
        lambda *refs: attend_kernel(rows, *refs),
        grid=(rows // tile,),
        in_specs=[
            pl.BlockSpec(memory_space=pltpu.SMEM),
            pl.BlockSpec((tile, 256), lambda i: (i, 0)),
            pl.BlockSpec((256, tile), lambda i: (0, i)),
            pl.BlockSpec((tile, 256), lambda i: (i, 0)),
            pl.BlockSpec((11, 2, tile), lambda i: (0, 0, i)),
        ]
        + [full(read.shape, 1) for read in reads],
        out_specs=pl.BlockSpec((tile, 256), lambda i: (i, 0)),
        out_shape=jax.ShapeDtypeStruct((rows, 256), BF16),
        scratch_shapes=[pltpu.VMEM((2, 640, 128), BF16)],
        compiler_params=pltpu.CompilerParams(vmem_limit_bytes=VMEM_LIMIT),
        cost_estimate=cost(3e9, 6 * MIB),
        name="attend",
    )(position, query, local, gg, codes, *reads)


def project_kernel(at_ref, a_ref, *refs):
    pieces, (out_ref, buf, acc_ref, sem) = refs[:-4], refs[-4:]
    x, core = at_ref[0] >> 1, at_ref[0] & 1
    copies = [pltpu.make_async_copy(piece, buf.at[p], sem.at[p]) for p, piece in enumerate(pieces)]
    half = len(pieces) // 2
    for p in range(half):
        copies[p].start()
        copies[p + half].start()
    for p in range(half):
        blocks, weights = [], []
        for flip in range(2):
            copies[p + flip * half].wait()
            blocks.append(a_ref[((x + (0, 3, 1, 2)[p]) & 3) * 2 + (core ^ flip)])
            weights.append(buf[p + flip * half])
        term = dot(jnp.concatenate(blocks, axis=1), jnp.concatenate(weights, axis=0))
        if p == 0:
            acc_ref[...] = term
        elif p < half - 1:
            acc_ref[...] += term
        else:
            out_ref[...] = (acc_ref[...] + term).astype(BF16)


def project(place, attended, pieces):
    rows = attended.shape[1]
    return pl.pallas_call(
        project_kernel,
        grid=(1,),
        in_specs=[pl.BlockSpec(memory_space=pltpu.SMEM), full(attended.shape, 1)]
        + [pl.BlockSpec(memory_space=pl.ANY)] * len(pieces),
        out_specs=full((rows, D), 1),
        out_shape=jax.ShapeDtypeStruct((rows, D), BF16),
        scratch_shapes=[
            pltpu.VMEM((len(pieces), 256, D), BF16),
            pltpu.VMEM((rows, D), F32),
            pltpu.SemaphoreType.DMA((len(pieces),)),
        ],
        compiler_params=pltpu.CompilerParams(vmem_limit_bytes=20 * MIB),
        cost_estimate=cost(2 * 256 * 2048 * 2048, 10 * MIB),
        name="project",
    )(place, attended, *pieces)


def body(tokens, w_proj, gain, level_codes, w_codes, block_exponent):
    place = lax.axis_index("mp").reshape(1)
    position = lax.axis_index("seq").reshape(1)

    def along_x(block, by):
        return lax.ppermute(block, "mp", [(m, (m // 2 + by) % 4 * 2 + m % 2) for m in range(8)])

    def other_core(block):
        return lax.ppermute(block, "mp", [(m, m ^ 1) for m in range(8)])

    def along_seq(block, to, senders=32):
        return lax.ppermute(block.astype(BF16), "seq", [(i, to(i)) for i in range(senders)])

    after = lax.optimization_barrier
    r = w_proj.reshape(D, 4, 2, 128).transpose(0, 2, 1, 3).reshape(D * 8, 128)

    weight = decode_weight(w_codes, block_exponent)
    gain, weight = after((gain, weight))
    from_left, from_right, from_far = along_x(weight, 1), along_x(weight, -1), along_x(weight, 2)
    keys, vt, query, gg, sr, state = projections(r, gain.reshape(1, 256), tokens)

    def inside(part, *earlier):
        return local_levels(part, query, keys, vt, level_codes, sr, *earlier)

    local, sums, reads = (), state.astype(F32), []
    for bit in range(4):
        read = along_seq(sums, lambda i: i ^ (1 << bit))
        local = (inside(bit, *local),)
        read, local = after((read, local))
        sums = sums + read.astype(F32)
        reads.append(read)
    reads.append(along_seq(sums, lambda i: 28 - i // 4 * 4 + i % 4, 16))
    attended = attend(position, query, *local, gg, level_codes, reads)
    attended, *pieces = after((attended, weight, from_left, from_right, from_far))
    attended = lax.all_to_all(attended.reshape(8, 256, 256), "mp", 0, 0, tiled=True)
    return project(place, attended, pieces + [other_core(piece) for piece in pieces])


def solution(mesh):
    placed = (
        P("seq", None),
        P(None, None, "mp"),
        P("mp"),
        P(None, "mp", "seq"),
        P("mp", None),
        P("mp", None),
    )
    return jax.shard_map(
        body, mesh=mesh, in_specs=placed, out_specs=P(("seq", "mp"), None), check_vma=False
    )
```

```python
import math

import jax
import jax.numpy as jnp
from jax import lax
from jax.experimental import pallas as pl
from jax.experimental.pallas import tpu as pltpu
from jax.sharding import PartitionSpec as P

D = 2048
HEAD_DIM = 128
STRETCH = 64
BLOCK = 128
TILE = 256
F32 = jnp.float32
BF16 = jnp.bfloat16
MIB = 1024 * 1024
VMEM_LIMIT = 60 * MIB


def cost(flops, size):
    return pl.CostEstimate(flops=int(flops), bytes_accessed=int(size), transcendentals=0)


def full(shape, buffers=2):
    zeros = (0,) * len(shape)
    return pl.BlockSpec(shape, lambda *_: zeros, pipeline_mode=pl.Buffered(buffers))


def dot(a, b):
    return jnp.dot(a, b, preferred_element_type=F32)


def dot_nt(a, b):
    return lax.dot_general(a, b, (((1,), (1,)), ((), ())), preferred_element_type=F32)


def decode_kernel(exponent_ref, codes_ref, out_ref):
    for block in range(codes_ref.shape[1] // BLOCK):
        lanes = slice(block * BLOCK, (block + 1) * BLOCK)
        codes = codes_ref[:, lanes]
        power = exponent_ref[pl.program_id(0), block] + 16
        scale = jnp.left_shift(jnp.int32(1), power).astype(F32) * jnp.float32(2.0 ** (-26))
        size = jnp.left_shift(8 + (codes & 7), (codes >> 3) & 15)
        size = jnp.where(codes >= 128, -size, size).astype(F32)
        out_ref[:, lanes] = (size * scale).astype(BF16)


def decode_weight(codes, exponents):
    rows = pl.BlockSpec((BLOCK, D), lambda i: (i, 0))
    return pl.pallas_call(
        decode_kernel,
        grid=(codes.shape[0] // BLOCK,),
        in_specs=[pl.BlockSpec(memory_space=pltpu.SMEM), rows],
        out_specs=rows,
        out_shape=jax.ShapeDtypeStruct(codes.shape, BF16),
        compiler_params=pltpu.CompilerParams(vmem_limit_bytes=VMEM_LIMIT),
        cost_estimate=cost(8e6, 3 * MIB),
        name="decode_weight",
    )(exponents, codes)


CHUNKS = 8
ROWS = 512
PARTS = (1, 2, 0, 3)


def unpack_chunk(chunk, parts, r_buf, w_ref, f_ref):
    size = r_buf.shape[0] // CHUNKS
    slot = chunk % f_ref.shape[0]
    f_ref[slot] = r_buf[pl.ds(chunk * size, size), :].astype(F32)
    rows = size // 8
    for at, part in enumerate(parts):
        for half in range(2):
            piece = f_ref[slot, pl.ds(half * 4 + part, rows, stride=8), :]
            w_ref[pl.ds(chunk * rows, rows), pl.ds(at * 256 + half * 128, 128)] = piece.astype(BF16)


def project_tiles(r_hbm, x_hbm, r_buf, x_buf, w_ref, f_ref, acc_ref, r_sem, x_sem, finish):
    size = r_buf.shape[0] // CHUNKS
    deep = w_ref.shape[0] // CHUNKS
    tiles = x_buf.shape[0] // ROWS

    def chunk_copy(chunk):
        at = pl.ds(chunk * size, size)
        return pltpu.make_async_copy(r_hbm.at[at], r_buf.at[at], r_sem.at[chunk])

    def tile_copy(tile):
        at = pl.ds(tile * ROWS, ROWS)
        return pltpu.make_async_copy(x_hbm.at[at], x_buf.at[at], x_sem.at[tile])

    r_copies = [chunk_copy(chunk) for chunk in range(CHUNKS)]
    x_copies = [tile_copy(tile) for tile in range(tiles)]
    for copy in r_copies[:2] + x_copies[:1] + r_copies[2:] + x_copies[1:]:
        copy.start()
    for chunk in range(2):
        r_copies[chunk].wait()
        unpack_chunk(chunk, PARTS, r_buf, w_ref, f_ref)
    x_copies[0].wait()
    for chunk in range(0, CHUNKS, 2):
        later = range(chunk + 2, min(chunk + 4, CHUNKS))
        for ahead in later:
            r_copies[ahead].wait()
        at = pl.ds(chunk * deep, 2 * deep)
        term = dot(x_buf[pl.ds(0, ROWS), at], w_ref[at, :])
        if chunk == 0:
            acc_ref[0] = term
        else:
            acc_ref[0] += term
        for ahead in later:
            unpack_chunk(ahead, PARTS, r_buf, w_ref, f_ref)
    for tile in range(1, tiles):
        x_copies[tile].wait()
        acc_ref[tile % 2] = dot(x_buf[pl.ds(tile * ROWS, ROWS), :], w_ref[...])
        finish(tile - 1)
    finish(tiles - 1)


def projection_scratch(rows):
    return [
        pltpu.VMEM((D * 8, 128), BF16),
        pltpu.VMEM((rows, D), BF16),
        pltpu.VMEM((D, 1024), BF16),
        pltpu.VMEM((2, D * 8 // CHUNKS, 128), F32),
        pltpu.VMEM((2, ROWS, 1024), F32),
        pltpu.SemaphoreType.DMA((CHUNKS,)),
        pltpu.SemaphoreType.DMA((rows // ROWS,)),
    ]


def projections_kernel(r_hbm, gain_ref, x_hbm, k_hbm, vt_hbm, q_hbm, gg_hbm, sr_ref, tot_ref, *scratch):
    *shared, k_buf, vt_buf, q_buf, gg_buf, u_ref, out_sem = scratch
    acc_ref = shared[4]
    copies = []

    def finish(tile):
        rows = pl.ds(tile * ROWS, ROWS)
        keys = acc_ref[tile % 2, :, 0:256].astype(BF16)
        k_buf[rows, :] = keys
        vt = acc_ref[tile % 2, :, 256:512].T.astype(BF16)
        vt_buf[:, rows] = vt
        q_buf[rows, :] = acc_ref[tile % 2, :, 512:768].astype(BF16)
        g = acc_ref[tile % 2, :, 768:1024]
        gg_buf[rows, :] = (gain_ref[...] * (g / (1.0 + jnp.exp(-g)))).astype(BF16)
        for place, (source, target) in enumerate(
            (
                (k_buf.at[rows], k_hbm.at[rows]),
                (vt_buf.at[:, rows], vt_hbm.at[:, rows]),
                (q_buf.at[rows], q_hbm.at[rows]),
                (gg_buf.at[rows], gg_hbm.at[rows]),
            )
        ):
            copy = pltpu.make_async_copy(source, target, out_sem.at[tile, place])
            copy.start()
            copies.append(copy)
        for sub in range(ROWS // TILE):
            at = slice(sub * TILE, (sub + 1) * TILE)
            u = dot(vt[:, at], keys[at])
            for head in range(2):
                lanes = slice(head * 128, (head + 1) * 128)
                u_ref[tile * (ROWS // TILE) + sub, head] = u[lanes, lanes]

    project_tiles(r_hbm, x_hbm, *shared, finish)
    u01 = u_ref[0] + u_ref[1]
    u03 = u01 + (u_ref[2] + u_ref[3])
    u45 = u_ref[4] + u_ref[5]
    for at, tile in enumerate((0, 2, 4, 6)):
        sr_ref[at] = u_ref[tile].astype(BF16)
    sr_ref[4] = u01.astype(BF16)
    sr_ref[5] = u45.astype(BF16)
    sr_ref[6] = u03.astype(BF16)
    tot_ref[...] = (u03 + (u45 + (u_ref[6] + u_ref[7]))).astype(BF16)
    for copy in copies:
        copy.wait()


def projections(r, gain, tokens):
    rows = tokens.shape[0]
    anywhere = pl.BlockSpec(memory_space=pl.ANY)
    return pl.pallas_call(
        projections_kernel,
        grid=(1,),
        in_specs=[anywhere, full((1, 256), 1), anywhere],
        out_specs=[anywhere] * 4 + [full((7, 2, 128, 128), 1), full((2, 128, 128), 1)],
        out_shape=[
            jax.ShapeDtypeStruct((rows, 256), BF16),
            jax.ShapeDtypeStruct((256, rows), BF16),
            jax.ShapeDtypeStruct((rows, 256), BF16),
            jax.ShapeDtypeStruct((rows, 256), BF16),
            jax.ShapeDtypeStruct((7, 2, 128, 128), BF16),
            jax.ShapeDtypeStruct((2, 128, 128), BF16),
        ],
        scratch_shapes=projection_scratch(rows)
        + [
            pltpu.VMEM((rows, 256), BF16),
            pltpu.VMEM((256, rows), BF16),
            pltpu.VMEM((rows, 256), BF16),
            pltpu.VMEM((rows, 256), BF16),
            pltpu.VMEM((8, 2, 128, 128), F32),
            pltpu.SemaphoreType.DMA((rows // ROWS, 4)),
        ],
        compiler_params=pltpu.CompilerParams(vmem_limit_bytes=VMEM_LIMIT),
        cost_estimate=cost(2 * rows * D * 1024, 18 * MIB),
        name="projections",
    )(r, gain, tokens)


def level_scale(span):
    return 1.0 / (128.0 * math.sqrt(HEAD_DIM * span))


def local_kernel(start, picks, q_ref, k_ref, vt_ref, codes_ref, *rest):
    states, out_ref = dict(zip(picks, rest)), rest[-1]
    subs = q_ref.shape[0] // TILE
    s = lax.broadcasted_iota(jnp.int32, (TILE, TILE), 0)
    t = lax.broadcasted_iota(jnp.int32, (TILE, TILE), 1)
    gap = (t >> 6) - (s >> 6)
    inside = (gap == 0) & (s <= t)
    odd = (gap == 1) & ((t >> 6) & 1 == 1)
    second = ((t >> 7) - (s >> 7) == 1)
    for sub in range(subs):
        tile = start + sub
        at = slice(sub * TILE, (sub + 1) * TILE)
        flags = [float((tile >> bit) & 1) for bit in range(3)]
        reads = (tile >> 1, 4 + (tile >> 2), 6)
        for head in range(2):
            lanes = slice(head * 128, (head + 1) * 128)

            def row(level, span, head=head, at=at):
                return codes_ref[level, head : head + 1, at].astype(F32) * level_scale(span)

            left = jnp.concatenate(
                [k_ref[at, lanes]] + [states[r][0, head] for r, flag in zip(reads, flags) if flag], axis=0
            )
            product = dot_nt(left, q_ref[at, lanes])
            weight = jnp.where(
                inside,
                row(0, STRETCH),
                jnp.where(
                    odd, row(1, STRETCH), jnp.where(second, row(2, 2 * STRETCH), 0.0)
                ),
            )
            masked = (product[:TILE] * weight).astype(BF16)
            total = dot(vt_ref[lanes, at], masked)
            levels = [j for j in range(3) if flags[j]]
            for place, j in enumerate(levels):
                rows = slice(TILE + place * 128, TILE + (place + 1) * 128)
                total += row(3 + j, TILE << j) * product[rows]
            out_ref[lanes, at] = total.astype(BF16)


def local_levels(part, query, keys, vt, codes, sr, *earlier):
    rows = query.shape[0]
    picks = [part] + [4 + part // 2] * (part % 2) + [6] * (part // 2)
    return pl.pallas_call(
        lambda *refs: local_kernel(part * (ROWS // TILE), picks, *refs),
        grid=(1,),
        in_specs=[
            pl.BlockSpec((ROWS, 256), lambda i: (part, 0), pipeline_mode=pl.Buffered(1)),
            pl.BlockSpec((ROWS, 256), lambda i: (part, 0), pipeline_mode=pl.Buffered(1)),
            pl.BlockSpec((256, ROWS), lambda i: (0, part), pipeline_mode=pl.Buffered(1)),
            pl.BlockSpec((6, 2, ROWS), lambda i: (0, 0, part), pipeline_mode=pl.Buffered(1)),
        ]
        + [
            pl.BlockSpec((1, 2, 128, 128), lambda i, pick=pick: (pick, 0, 0, 0), pipeline_mode=pl.Buffered(1))
            for pick in picks
        ]
        + [pl.BlockSpec(memory_space=pl.ANY)] * len(earlier),
        out_specs=pl.BlockSpec((256, ROWS), lambda i: (0, part), pipeline_mode=pl.Buffered(1)),
        out_shape=jax.ShapeDtypeStruct((256, rows), BF16),
        input_output_aliases={4 + len(picks): 0} if earlier else {},
        compiler_params=pltpu.CompilerParams(vmem_limit_bytes=VMEM_LIMIT),
        cost_estimate=cost(3e9, 2 * MIB),
        name=f"local_levels_{part}",
    )(query, keys, vt, codes, *[sr] * len(picks), *earlier)


def attend_kernel(rows_here, at_ref, q_ref, m_ref, gg_ref, codes_ref, *refs):
    *read_refs, out_ref, sd_ref = refs
    position = at_ref[0]

    @pl.when(pl.program_id(0) == 0)
    def _():
        for j, read_ref in enumerate(read_refs):
            for head in range(2):
                sd_ref[head, pl.ds(j * 128, 128), :] = read_ref[head]

    for head in range(2):
        lanes = slice(head * 128, (head + 1) * 128)
        product = dot_nt(sd_ref[head], q_ref[:, lanes])
        memory = m_ref[lanes, :].astype(F32)
        for j in range(5):
            scale = ((position >> j) & 1).astype(F32) * level_scale(rows_here << j)
            row = codes_ref[6 + j, head : head + 1, :].astype(F32) * scale
            memory += row * product[j * 128 : (j + 1) * 128]
        mean = jnp.mean(memory * memory, axis=0, keepdims=True)
        normed = memory * lax.rsqrt(mean + 1e-06)
        out_ref[:, lanes] = (normed.T * gg_ref[:, lanes].astype(F32)).astype(BF16)


def attend(position, query, local, gg, codes, reads):
    rows = query.shape[0]
    tile = 1024
    return pl.pallas_call(
        lambda *refs: attend_kernel(rows, *refs),
        grid=(rows // tile,),
        in_specs=[
            pl.BlockSpec(memory_space=pltpu.SMEM),
            pl.BlockSpec((tile, 256), lambda i: (i, 0)),
            pl.BlockSpec((256, tile), lambda i: (0, i)),
            pl.BlockSpec((tile, 256), lambda i: (i, 0)),
            pl.BlockSpec((11, 2, tile), lambda i: (0, 0, i)),
        ]
        + [full(read.shape, 1) for read in reads],
        out_specs=pl.BlockSpec((tile, 256), lambda i: (i, 0)),
        out_shape=jax.ShapeDtypeStruct((rows, 256), BF16),
        scratch_shapes=[pltpu.VMEM((2, 640, 128), BF16)],
        compiler_params=pltpu.CompilerParams(vmem_limit_bytes=VMEM_LIMIT),
        cost_estimate=cost(3e9, 6 * MIB),
        name="attend",
    )(position, query, local, gg, codes, *reads)


def project_kernel(at_ref, a_ref, *refs):
    pieces, (out_ref, buf, acc_ref, sem) = refs[:-4], refs[-4:]
    x, core = at_ref[0] >> 1, at_ref[0] & 1
    copies = [pltpu.make_async_copy(piece, buf.at[p], sem.at[p]) for p, piece in enumerate(pieces)]
    half = len(pieces) // 2
    for p in range(half):
        copies[p].start()
        copies[p + half].start()
    for p in range(half):
        blocks, weights = [], []
        for flip in range(2):
            copies[p + flip * half].wait()
            blocks.append(a_ref[((x + (0, 3, 1, 2)[p]) & 3) * 2 + (core ^ flip)])
            weights.append(buf[p + flip * half])
        term = dot(jnp.concatenate(blocks, axis=1), jnp.concatenate(weights, axis=0))
        if p == 0:
            acc_ref[...] = term
        elif p < half - 1:
            acc_ref[...] += term
        else:
            out_ref[...] = (acc_ref[...] + term).astype(BF16)


def project(place, attended, pieces):
    rows = attended.shape[1]
    return pl.pallas_call(
        project_kernel,
        grid=(1,),
        in_specs=[pl.BlockSpec(memory_space=pltpu.SMEM), full(attended.shape, 1)]
        + [pl.BlockSpec(memory_space=pl.ANY)] * len(pieces),
        out_specs=full((rows, D), 1),
        out_shape=jax.ShapeDtypeStruct((rows, D), BF16),
        scratch_shapes=[
            pltpu.VMEM((len(pieces), 256, D), BF16),
            pltpu.VMEM((rows, D), F32),
            pltpu.SemaphoreType.DMA((len(pieces),)),
        ],
        compiler_params=pltpu.CompilerParams(vmem_limit_bytes=20 * MIB),
        cost_estimate=cost(2 * 256 * 2048 * 2048, 10 * MIB),
        name="project",
    )(place, attended, *pieces)


def body(tokens, w_proj, gain, level_codes, w_codes, block_exponent):
    place = lax.axis_index("mp").reshape(1)
    position = lax.axis_index("seq").reshape(1)

    def along_x(block, by):
        return lax.ppermute(block, "mp", [(m, (m // 2 + by) % 4 * 2 + m % 2) for m in range(8)])

    def other_core(block):
        return lax.ppermute(block, "mp", [(m, m ^ 1) for m in range(8)])

    def along_seq(block, to, senders=32):
        return lax.ppermute(block.astype(BF16), "seq", [(i, to(i)) for i in range(senders)])

    after = lax.optimization_barrier
    r = w_proj.reshape(D, 4, 2, 128).transpose(0, 2, 1, 3).reshape(D * 8, 128)

    weight = decode_weight(w_codes, block_exponent)
    gain, weight = after((gain, weight))
    from_left, from_right, from_far = along_x(weight, 1), along_x(weight, -1), along_x(weight, 2)
    keys, vt, query, gg, sr, state = projections(r, gain.reshape(1, 256), tokens)

    def inside(part, *earlier):
        return local_levels(part, query, keys, vt, level_codes, sr, *earlier)

    local, sums, reads = (), state.astype(F32), []
    for bit in range(4):
        read = along_seq(sums, lambda i: i ^ (1 << bit))
        local = (inside(bit, *local),)
        read, local = after((read, local))
        sums = sums + read.astype(F32)
        reads.append(read)
    reads.append(along_seq(sums, lambda i: 28 - i // 4 * 4 + i % 4, 16))
    attended = attend(position, query, *local, gg, level_codes, reads)
    attended, *pieces = after((attended, weight, from_left, from_right, from_far))
    attended = lax.all_to_all(attended.reshape(8, 256, 256), "mp", 0, 0, tiled=True)
    return project(place, attended, pieces + [other_core(piece) for piece in pieces])


def solution(mesh):
    placed = (
        P("seq", None),
        P(None, None, "mp"),
        P("mp"),
        P(None, "mp", "seq"),
        P("mp", None),
        P("mp", None),
    )
    return jax.shard_map(
        body, mesh=mesh, in_specs=placed, out_specs=P(("seq", "mp"), None), check_vma=False
    )
```

```python
import math

import jax
import jax.numpy as jnp
from jax import lax
from jax.experimental import pallas as pl
from jax.experimental.pallas import tpu as pltpu
from jax.sharding import PartitionSpec as P

D = 2048
HEAD_DIM = 128
STRETCH = 64
BLOCK = 128
TILE = 256
F32 = jnp.float32
BF16 = jnp.bfloat16
MIB = 1024 * 1024
VMEM_LIMIT = 60 * MIB


def cost(flops, size):
    return pl.CostEstimate(flops=int(flops), bytes_accessed=int(size), transcendentals=0)


def full(shape, buffers=2):
    zeros = (0,) * len(shape)
    return pl.BlockSpec(shape, lambda *_: zeros, pipeline_mode=pl.Buffered(buffers))


def dot(a, b):
    return jnp.dot(a, b, preferred_element_type=F32)


def dot_nt(a, b):
    return lax.dot_general(a, b, (((1,), (1,)), ((), ())), preferred_element_type=F32)


def decode_kernel(exponent_ref, codes_ref, out_ref):
    for block in range(codes_ref.shape[1] // BLOCK):
        lanes = slice(block * BLOCK, (block + 1) * BLOCK)
        codes = codes_ref[:, lanes]
        power = exponent_ref[pl.program_id(0), block] + 16
        scale = jnp.left_shift(jnp.int32(1), power).astype(F32) * jnp.float32(2.0 ** (-26))
        size = jnp.left_shift(8 + (codes & 7), (codes >> 3) & 15)
        size = jnp.where(codes >= 128, -size, size).astype(F32)
        out_ref[:, lanes] = (size * scale).astype(BF16)


def decode_weight(codes, exponents):
    rows = pl.BlockSpec((BLOCK, D), lambda i: (i, 0))
    return pl.pallas_call(
        decode_kernel,
        grid=(codes.shape[0] // BLOCK,),
        in_specs=[pl.BlockSpec(memory_space=pltpu.SMEM), rows],
        out_specs=rows,
        out_shape=jax.ShapeDtypeStruct(codes.shape, BF16),
        compiler_params=pltpu.CompilerParams(vmem_limit_bytes=VMEM_LIMIT),
        cost_estimate=cost(8e6, 3 * MIB),
        name="decode_weight",
    )(exponents, codes)


CHUNKS = 8
ROWS = 512
PARTS = (1, 2, 0, 3)


def unpack_chunk(chunk, parts, r_buf, w_ref, f_ref):
    size = r_buf.shape[0] // CHUNKS
    slot = chunk % f_ref.shape[0]
    f_ref[slot] = r_buf[pl.ds(chunk * size, size), :].astype(F32)
    rows = size // 8
    for at, part in enumerate(parts):
        for half in range(2):
            piece = f_ref[slot, pl.ds(half * 4 + part, rows, stride=8), :]
            w_ref[pl.ds(chunk * rows, rows), pl.ds(at * 256 + half * 128, 128)] = piece.astype(BF16)


def project_tiles(r_hbm, x_hbm, r_buf, x_buf, w_ref, f_ref, acc_ref, r_sem, x_sem, finish):
    size = r_buf.shape[0] // CHUNKS
    deep = w_ref.shape[0] // CHUNKS
    tiles = x_buf.shape[0] // ROWS

    def chunk_copy(chunk):
        at = pl.ds(chunk * size, size)
        return pltpu.make_async_copy(r_hbm.at[at], r_buf.at[at], r_sem.at[chunk])

    def tile_copy(tile):
        at = pl.ds(tile * ROWS, ROWS)
        return pltpu.make_async_copy(x_hbm.at[at], x_buf.at[at], x_sem.at[tile])

    r_copies = [chunk_copy(chunk) for chunk in range(CHUNKS)]
    x_copies = [tile_copy(tile) for tile in range(tiles)]
    for copy in r_copies[:4] + x_copies[:1] + r_copies[4:] + x_copies[1:]:
        copy.start()
    for chunk in range(2):
        r_copies[chunk].wait()
        unpack_chunk(chunk, PARTS, r_buf, w_ref, f_ref)
    x_copies[0].wait()
    for chunk in range(0, CHUNKS, 2):
        later = range(chunk + 2, min(chunk + 4, CHUNKS))
        for ahead in later:
            r_copies[ahead].wait()
        at = pl.ds(chunk * deep, 2 * deep)
        term = dot(x_buf[pl.ds(0, ROWS), at], w_ref[at, :])
        if chunk == 0:
            acc_ref[0] = term
        else:
            acc_ref[0] += term
        for ahead in later:
            unpack_chunk(ahead, PARTS, r_buf, w_ref, f_ref)
    for tile in range(1, tiles):
        x_copies[tile].wait()
        acc_ref[tile % 2] = dot(x_buf[pl.ds(tile * ROWS, ROWS), :], w_ref[...])
        finish(tile - 1)
    finish(tiles - 1)


def projection_scratch(rows):
    return [
        pltpu.VMEM((D * 8, 128), BF16),
        pltpu.VMEM((rows, D), BF16),
        pltpu.VMEM((D, 1024), BF16),
        pltpu.VMEM((2, D * 8 // CHUNKS, 128), F32),
        pltpu.VMEM((2, ROWS, 1024), F32),
        pltpu.SemaphoreType.DMA((CHUNKS,)),
        pltpu.SemaphoreType.DMA((rows // ROWS,)),
    ]


def projections_kernel(r_hbm, gain_ref, x_hbm, k_hbm, vt_hbm, q_hbm, gg_hbm, sr_ref, tot_ref, *scratch):
    *shared, k_buf, vt_buf, q_buf, gg_buf, u_ref, out_sem = scratch
    acc_ref = shared[4]
    copies = []

    def finish(tile):
        rows = pl.ds(tile * ROWS, ROWS)
        keys = acc_ref[tile % 2, :, 0:256].astype(BF16)
        k_buf[rows, :] = keys
        vt = acc_ref[tile % 2, :, 256:512].T.astype(BF16)
        vt_buf[:, rows] = vt
        q_buf[rows, :] = acc_ref[tile % 2, :, 512:768].astype(BF16)
        g = acc_ref[tile % 2, :, 768:1024]
        gg_buf[rows, :] = (gain_ref[...] * (g / (1.0 + jnp.exp(-g)))).astype(BF16)
        for place, (source, target) in enumerate(
            (
                (k_buf.at[rows], k_hbm.at[rows]),
                (vt_buf.at[:, rows], vt_hbm.at[:, rows]),
                (q_buf.at[rows], q_hbm.at[rows]),
                (gg_buf.at[rows], gg_hbm.at[rows]),
            )
        ):
            copy = pltpu.make_async_copy(source, target, out_sem.at[tile, place])
            copy.start()
            copies.append(copy)
        for sub in range(ROWS // TILE):
            at = slice(sub * TILE, (sub + 1) * TILE)
            u = dot(vt[:, at], keys[at])
            for head in range(2):
                lanes = slice(head * 128, (head + 1) * 128)
                u_ref[tile * (ROWS // TILE) + sub, head] = u[lanes, lanes]

    project_tiles(r_hbm, x_hbm, *shared, finish)
    u01 = u_ref[0] + u_ref[1]
    u03 = u01 + (u_ref[2] + u_ref[3])
    u45 = u_ref[4] + u_ref[5]
    for at, tile in enumerate((0, 2, 4, 6)):
        sr_ref[at] = u_ref[tile].astype(BF16)
    sr_ref[4] = u01.astype(BF16)
    sr_ref[5] = u45.astype(BF16)
    sr_ref[6] = u03.astype(BF16)
    tot_ref[...] = (u03 + (u45 + (u_ref[6] + u_ref[7]))).astype(BF16)
    for copy in copies:
        copy.wait()


def projections(r, gain, tokens):
    rows = tokens.shape[0]
    anywhere = pl.BlockSpec(memory_space=pl.ANY)
    return pl.pallas_call(
        projections_kernel,
        grid=(1,),
        in_specs=[anywhere, full((1, 256), 1), anywhere],
        out_specs=[anywhere] * 4 + [full((7, 2, 128, 128), 1), full((2, 128, 128), 1)],
        out_shape=[
            jax.ShapeDtypeStruct((rows, 256), BF16),
            jax.ShapeDtypeStruct((256, rows), BF16),
            jax.ShapeDtypeStruct((rows, 256), BF16),
            jax.ShapeDtypeStruct((rows, 256), BF16),
            jax.ShapeDtypeStruct((7, 2, 128, 128), BF16),
            jax.ShapeDtypeStruct((2, 128, 128), BF16),
        ],
        scratch_shapes=projection_scratch(rows)
        + [
            pltpu.VMEM((rows, 256), BF16),
            pltpu.VMEM((256, rows), BF16),
            pltpu.VMEM((rows, 256), BF16),
            pltpu.VMEM((rows, 256), BF16),
            pltpu.VMEM((8, 2, 128, 128), F32),
            pltpu.SemaphoreType.DMA((rows // ROWS, 4)),
        ],
        compiler_params=pltpu.CompilerParams(vmem_limit_bytes=VMEM_LIMIT),
        cost_estimate=cost(2 * rows * D * 1024, 18 * MIB),
        name="projections",
    )(r, gain, tokens)


def level_scale(span):
    return 1.0 / (128.0 * math.sqrt(HEAD_DIM * span))


def local_kernel(start, picks, q_ref, k_ref, vt_ref, codes_ref, *rest):
    states, out_ref = dict(zip(picks, rest)), rest[-1]
    subs = q_ref.shape[0] // TILE
    s = lax.broadcasted_iota(jnp.int32, (TILE, TILE), 0)
    t = lax.broadcasted_iota(jnp.int32, (TILE, TILE), 1)
    gap = (t >> 6) - (s >> 6)
    inside = (gap == 0) & (s <= t)
    odd = (gap == 1) & ((t >> 6) & 1 == 1)
    second = ((t >> 7) - (s >> 7) == 1)
    for sub in range(subs):
        tile = start + sub
        at = slice(sub * TILE, (sub + 1) * TILE)
        flags = [float((tile >> bit) & 1) for bit in range(3)]
        reads = (tile >> 1, 4 + (tile >> 2), 6)
        for head in range(2):
            lanes = slice(head * 128, (head + 1) * 128)

            def row(level, span, head=head, at=at):
                return codes_ref[level, head : head + 1, at].astype(F32) * level_scale(span)

            left = jnp.concatenate(
                [k_ref[at, lanes]] + [states[r][0, head] for r, flag in zip(reads, flags) if flag], axis=0
            )
            product = dot_nt(left, q_ref[at, lanes])
            weight = jnp.where(
                inside,
                row(0, STRETCH),
                jnp.where(
                    odd, row(1, STRETCH), jnp.where(second, row(2, 2 * STRETCH), 0.0)
                ),
            )
            masked = (product[:TILE] * weight).astype(BF16)
            total = dot(vt_ref[lanes, at], masked)
            levels = [j for j in range(3) if flags[j]]
            for place, j in enumerate(levels):
                rows = slice(TILE + place * 128, TILE + (place + 1) * 128)
                total += row(3 + j, TILE << j) * product[rows]
            out_ref[lanes, at] = total.astype(BF16)


def local_levels(part, query, keys, vt, codes, sr, *earlier):
    rows = query.shape[0]
    picks = [part] + [4 + part // 2] * (part % 2) + [6] * (part // 2)
    return pl.pallas_call(
        lambda *refs: local_kernel(part * (ROWS // TILE), picks, *refs),
        grid=(1,),
        in_specs=[
            pl.BlockSpec((ROWS, 256), lambda i: (part, 0), pipeline_mode=pl.Buffered(1)),
            pl.BlockSpec((ROWS, 256), lambda i: (part, 0), pipeline_mode=pl.Buffered(1)),
            pl.BlockSpec((256, ROWS), lambda i: (0, part), pipeline_mode=pl.Buffered(1)),
            pl.BlockSpec((11, 2, ROWS), lambda i: (0, 0, part), pipeline_mode=pl.Buffered(1)),
        ]
        + [
            pl.BlockSpec((1, 2, 128, 128), lambda i, pick=pick: (pick, 0, 0, 0), pipeline_mode=pl.Buffered(1))
            for pick in picks
        ]
        + [pl.BlockSpec(memory_space=pl.ANY)] * len(earlier),
        out_specs=pl.BlockSpec((256, ROWS), lambda i: (0, part), pipeline_mode=pl.Buffered(1)),
        out_shape=jax.ShapeDtypeStruct((256, rows), BF16),
        input_output_aliases={4 + len(picks): 0} if earlier else {},
        compiler_params=pltpu.CompilerParams(vmem_limit_bytes=VMEM_LIMIT),
        cost_estimate=cost(3e9, 2 * MIB),
        name=f"local_levels_{part}",
    )(query, keys, vt, codes, *[sr] * len(picks), *earlier)


def attend_kernel(rows_here, at_ref, q_ref, m_ref, gg_ref, codes_ref, *refs):
    *read_refs, out_ref, sd_ref = refs
    position = at_ref[0]

    @pl.when(pl.program_id(0) == 0)
    def _():
        for j, read_ref in enumerate(read_refs):
            for head in range(2):
                sd_ref[head, pl.ds(j * 128, 128), :] = read_ref[head]

    for head in range(2):
        lanes = slice(head * 128, (head + 1) * 128)
        product = dot_nt(sd_ref[head], q_ref[:, lanes])
        memory = m_ref[lanes, :].astype(F32)
        for j in range(5):
            scale = ((position >> j) & 1).astype(F32) * level_scale(rows_here << j)
            row = codes_ref[6 + j, head : head + 1, :].astype(F32) * scale
            memory += row * product[j * 128 : (j + 1) * 128]
        mean = jnp.mean(memory * memory, axis=0, keepdims=True)
        normed = memory * lax.rsqrt(mean + 1e-06)
        out_ref[:, lanes] = (normed.T * gg_ref[:, lanes].astype(F32)).astype(BF16)


def attend(position, query, local, gg, codes, reads):
    rows = query.shape[0]
    tile = 1024
    return pl.pallas_call(
        lambda *refs: attend_kernel(rows, *refs),
        grid=(rows // tile,),
        in_specs=[
            pl.BlockSpec(memory_space=pltpu.SMEM),
            pl.BlockSpec((tile, 256), lambda i: (i, 0)),
            pl.BlockSpec((256, tile), lambda i: (0, i)),
            pl.BlockSpec((tile, 256), lambda i: (i, 0)),
            pl.BlockSpec((11, 2, tile), lambda i: (0, 0, i)),
        ]
        + [full(read.shape, 1) for read in reads],
        out_specs=pl.BlockSpec((tile, 256), lambda i: (i, 0)),
        out_shape=jax.ShapeDtypeStruct((rows, 256), BF16),
        scratch_shapes=[pltpu.VMEM((2, 640, 128), BF16)],
        compiler_params=pltpu.CompilerParams(vmem_limit_bytes=VMEM_LIMIT),
        cost_estimate=cost(3e9, 6 * MIB),
        name="attend",
    )(position, query, local, gg, codes, *reads)


def project_kernel(at_ref, a_ref, *refs):
    pieces, (out_ref, buf, acc_ref, sem) = refs[:-4], refs[-4:]
    x, core = at_ref[0] >> 1, at_ref[0] & 1
    copies = [pltpu.make_async_copy(piece, buf.at[p], sem.at[p]) for p, piece in enumerate(pieces)]
    half = len(pieces) // 2
    for p in range(half):
        copies[p].start()
        copies[p + half].start()
    for p in range(half):
        blocks, weights = [], []
        for flip in range(2):
            copies[p + flip * half].wait()
            blocks.append(a_ref[((x + (0, 3, 1, 2)[p]) & 3) * 2 + (core ^ flip)])
            weights.append(buf[p + flip * half])
        term = dot(jnp.concatenate(blocks, axis=1), jnp.concatenate(weights, axis=0))
        if p == 0:
            acc_ref[...] = term
        elif p < half - 1:
            acc_ref[...] += term
        else:
            out_ref[...] = (acc_ref[...] + term).astype(BF16)


def project(place, attended, pieces):
    rows = attended.shape[1]
    return pl.pallas_call(
        project_kernel,
        grid=(1,),
        in_specs=[pl.BlockSpec(memory_space=pltpu.SMEM), full(attended.shape, 1)]
        + [pl.BlockSpec(memory_space=pl.ANY)] * len(pieces),
        out_specs=full((rows, D), 1),
        out_shape=jax.ShapeDtypeStruct((rows, D), BF16),
        scratch_shapes=[
            pltpu.VMEM((len(pieces), 256, D), BF16),
            pltpu.VMEM((rows, D), F32),
            pltpu.SemaphoreType.DMA((len(pieces),)),
        ],
        compiler_params=pltpu.CompilerParams(vmem_limit_bytes=20 * MIB),
        cost_estimate=cost(2 * 256 * 2048 * 2048, 10 * MIB),
        name="project",
    )(place, attended, *pieces)


def body(tokens, w_proj, gain, level_codes, w_codes, block_exponent):
    place = lax.axis_index("mp").reshape(1)
    position = lax.axis_index("seq").reshape(1)

    def along_x(block, by):
        return lax.ppermute(block, "mp", [(m, (m // 2 + by) % 4 * 2 + m % 2) for m in range(8)])

    def other_core(block):
        return lax.ppermute(block, "mp", [(m, m ^ 1) for m in range(8)])

    def along_seq(block, to, senders=32):
        return lax.ppermute(block.astype(BF16), "seq", [(i, to(i)) for i in range(senders)])

    after = lax.optimization_barrier
    r = w_proj.reshape(D, 4, 2, 128).transpose(0, 2, 1, 3).reshape(D * 8, 128)

    weight = decode_weight(w_codes, block_exponent)
    gain, weight = after((gain, weight))
    from_left, from_right, from_far = along_x(weight, 1), along_x(weight, -1), along_x(weight, 2)
    keys, vt, query, gg, sr, state = projections(r, gain.reshape(1, 256), tokens)

    def inside(part, *earlier):
        return local_levels(part, query, keys, vt, level_codes, sr, *earlier)

    local, sums, reads = (), state.astype(F32), []
    for bit in range(4):
        read = along_seq(sums, lambda i: i ^ (1 << bit))
        local = (inside(bit, *local),)
        read, local = after((read, local))
        sums = sums + read.astype(F32)
        reads.append(read)
    reads.append(along_seq(sums, lambda i: 28 - i // 4 * 4 + i % 4, 16))
    attended = attend(position, query, *local, gg, level_codes, reads)
    attended, *pieces = after((attended, weight, from_left, from_right, from_far))
    attended = lax.all_to_all(attended.reshape(8, 256, 256), "mp", 0, 0, tiled=True)
    return project(place, attended, pieces + [other_core(piece) for piece in pieces])


def solution(mesh):
    placed = (
        P("seq", None),
        P(None, None, "mp"),
        P("mp"),
        P(None, "mp", "seq"),
        P("mp", None),
        P("mp", None),
    )
    return jax.shard_map(
        body, mesh=mesh, in_specs=placed, out_specs=P(("seq", "mp"), None), check_vma=False
    )
```
